256 devices in a mesh: blk: 128 (over z_hi, y, x, core), head: 2 (over z_lo).
Axes of the slice: x: 4, y: 4, z: 8 (z_hi: 4, z_lo: 2; z = z_hi * 2 + z_lo), core: 2. Of those that a mesh axis runs over, the one named last changes fastest.
Arguments:
- cells: bfloat16 [65536, 256], P('blk', 'head'), may hold values from -6 to 6
- w_query: bfloat16 [256, 256], P(None, 'head'), may hold values from -0.375 to 0.375
- w_key: bfloat16 [256, 256], P(None, 'head'), may hold values from -0.375 to 0.375
- w_value: bfloat16 [256, 256], P(None, 'head'), may hold values from -0.375 to 0.375
- w_source: bfloat16 [2, 256, 256], P(None, None, 'head'), may hold values from -0.375 to 0.375
- w_target: bfloat16 [2, 256, 256], P(None, None, 'head'), may hold values from -0.375 to 0.375
- msg_bias: float32 [2, 256], P(None, 'head'), may hold values from -3 to 3
- w_out: bfloat16 [256, 256], P('head'), may hold values from -0.375 to 0.375
- nbr_block: int32 [512, 4], P('blk'), may hold values from 0 to 511, as said below
- edge_src: int32 [65536, 8], P('blk'), may hold values from 0 to 511
- key_blocks: int32 [512, 32], P('blk'), may hold values from 0 to 511, as said below
Outputs:
- updated: bfloat16 [65536, 256], P('blk', 'head')
The draws below stay inside these ranges and needn't reach their ends.
Inputs may be any that keep to these rules, and one draw needn't show every extreme that they name: `nbr_block`: the source blocks listed for a destination block lie in its own partition of 4 consecutive blocks or in the partition just before or after it on the loop of 128 partitions. `key_blocks`: each row lists 32 key blocks from 32 different partitions; among all key blocks listed by the 4 query blocks of one partition, those that lie in one partition are the same block.
All inputs are finite; a program needn't handle non-finite values.
Results may differ from the reference program's by a relative error of at most 0.0015.
The reference program's roundings to bfloat16 on the way (of `source` and `mixed`) count: a program that leaves them out, or rounds other values in their place, can miss the bound.
Values may be sent and summed in bfloat16 or wider, within the bound.
No kernel may reach another device: no remote copies, remote signals or barrier semaphores. Data moves between devices by JAX's collectives and lax.ppermute only.
A program may use at most 128 MiB of HBM per device.

```python
import jax
import jax.numpy as jnp
from jax import lax

D = 256
HEADS = 8
HEAD_DIM = 32
BLOCK = 128
EDGES = 8
NBB = 4
KB = 32
BLK_DEV = 4
CELLS = 65536
BLOCKS = 512
N_BLK = 128


def draw_nbr_block(key, part):
    blocks = jnp.arange(BLOCKS, dtype=jnp.int32)
    home = blocks // BLK_DEV
    offset = jax.random.randint(jax.random.fold_in(key, 11), (BLOCKS, NBB), -1, 2)
    local = jax.random.randint(jax.random.fold_in(key, 12), (BLOCKS, NBB), 0, BLK_DEV)
    return ((home[:, None] + offset) % N_BLK * BLK_DEV + local).astype(jnp.int32)


def draw_key_blocks(key, part):
    table = jax.random.randint(jax.random.fold_in(key, 21), (N_BLK, N_BLK), 0, BLK_DEV)
    base = jax.random.fold_in(key, 22)

    def one_row(block):
        chosen = jax.random.permutation(jax.random.fold_in(base, block), N_BLK)[:KB]
        return chosen * BLK_DEV + table[block // BLK_DEV, chosen]
    return jax.vmap(one_row)(jnp.arange(BLOCKS, dtype=jnp.int32)).astype(jnp.int32)


def touch_ends(drawn, rng, least, top_value):
    longest = drawn.shape.index(max(drawn.shape))
    spots = []
    for shift in (0, 1):
        where = [jax.random.randint(jax.random.fold_in(rng, axis), (), 0, length) for axis, length in enumerate(drawn.shape)]
        where[longest] = (where[longest] + shift) % drawn.shape[longest]
        spots.append(tuple(where))
    return drawn.at[spots[0]].set(least).at[spots[1]].set(top_value)


def shard_levels(stream_key, shape, shards, low, largest):
    def one(axis_at, blocks):
        steps = jax.random.uniform(jax.random.fold_in(jax.random.fold_in(stream_key, 6), axis_at), (blocks,), jnp.float32, low / len(shards), largest / len(shards))
        return jnp.repeat(jnp.exp(steps), shape[axis_at] // blocks).reshape((-1,) + (1,) * (len(shape) - axis_at - 1))

    gain = one(*shards[0])
    for cut in shards[1:]:
        gain = gain * one(*cut)
    return gain


def normal_values(key, shape, deviation, bound, split=(), kind=jnp.bfloat16):
    gain = shard_levels(key, shape, split, -0.22, 0.18) if split else 1.0
    array = jax.random.normal(key, shape, jnp.float32) * deviation * gain
    return jnp.minimum(jnp.maximum(array, -bound), bound).astype(kind)


def setup_inputs(seed: int = 0) -> dict:
    streams_of = jax.random.split(jax.random.key(seed), 12)
    cells = normal_values(streams_of[0], (CELLS, D), 1.0, 6.0, ((0, 128), (1, 2)))
    w_query = normal_values(streams_of[1], (D, D), D ** -0.5, 0.375, ((1, 2),))
    w_key = normal_values(streams_of[2], (D, D), D ** -0.5, 0.375, ((1, 2),))
    w_value = normal_values(streams_of[3], (D, D), D ** -0.5, 0.375, ((1, 2),))
    w_source = normal_values(streams_of[4], (2, D, D), D ** -0.5, 0.375, ((2, 2),))
    w_target = normal_values(streams_of[5], (2, D, D), D ** -0.5, 0.375, ((2, 2),))
    msg_bias = normal_values(streams_of[6], (2, D), 0.5, 3.0, ((1, 2),), jnp.float32)
    w_out = normal_values(streams_of[7], (D, D), D ** -0.5, 0.375, ((0, 2),))
    nbr_block = draw_nbr_block(jax.random.fold_in(streams_of[11], 71), 0)
    edge_src = touch_ends(jax.random.randint(streams_of[9], (CELLS, EDGES), 0, NBB * BLOCK), jax.random.fold_in(streams_of[9], 1), 0, (NBB * BLOCK) - 1).astype(jnp.int32)
    key_blocks = draw_key_blocks(jax.random.fold_in(streams_of[11], 71), 0)
    return dict(cells=cells, w_query=w_query, w_key=w_key, w_value=w_value, w_source=w_source, w_target=w_target, msg_bias=msg_bias, w_out=w_out, nbr_block=nbr_block, edge_src=edge_src, key_blocks=key_blocks)


def reference(cells, w_query, w_key, w_value, w_source, w_target, msg_bias, w_out, nbr_block, edge_src, key_blocks):
    count = cells.shape[0]
    queries = jnp.dot(cells, w_query, preferred_element_type=jnp.float32).astype(jnp.bfloat16)
    keys = jnp.dot(cells, w_key, preferred_element_type=jnp.float32).astype(jnp.bfloat16)
    values = jnp.dot(cells, w_value, preferred_element_type=jnp.float32).astype(jnp.bfloat16)
    source = jnp.einsum("cd,gdk->cgk", cells.astype(jnp.float32), w_source.astype(jnp.float32)).astype(jnp.bfloat16)
    target = jnp.einsum("cd,gdk->cgk", cells.astype(jnp.float32), w_target.astype(jnp.float32)) + msg_bias[None]
    own = (jnp.arange(count, dtype=jnp.int32) // BLOCK).astype(jnp.int32)
    src_block = nbr_block[own[:, None], edge_src // BLOCK]
    index = (src_block * BLOCK + edge_src % BLOCK).astype(jnp.int32)
    pre = source[index].astype(jnp.float32) + target[:, None]
    message = jax.nn.sigmoid(pre[:, :, 0]) * jax.nn.silu(pre[:, :, 1])
    aggregate = jnp.mean(message, axis=1)
    scale = HEAD_DIM ** -0.5

    def one_block(block):
        start = (block * BLOCK).astype(jnp.int32)
        query = lax.dynamic_slice_in_dim(queries, start, BLOCK, 0).astype(jnp.float32).reshape(BLOCK, HEADS, HEAD_DIM)
        rows = (key_blocks[block][:, None] * BLOCK + jnp.arange(BLOCK, dtype=jnp.int32)[None, :]).reshape(-1)
        key = keys[rows].astype(jnp.float32).reshape(-1, HEADS, HEAD_DIM)
        value = values[rows].astype(jnp.float32).reshape(-1, HEADS, HEAD_DIM)
        scores = jnp.einsum("qhd,khd->hqk", query, key) * scale
        weight = jnp.exp(scores)
        total = jnp.sum(weight, axis=2)
        numer = jnp.einsum("hqk,khd->qhd", weight.astype(jnp.bfloat16).astype(jnp.float32), value)
        return (numer / jnp.transpose(total)[:, :, None]).reshape(BLOCK, HEADS * HEAD_DIM)

    mixed = lax.map(one_block, jnp.arange(count // BLOCK, dtype=jnp.int32))
    mixed = mixed.reshape(count, HEADS * HEAD_DIM).astype(jnp.bfloat16)
    attended = jnp.dot(mixed, w_out, preferred_element_type=jnp.float32)
    return (cells.astype(jnp.float32) + aggregate + attended).astype(jnp.bfloat16)
```

```python
import functools
import math

import jax
import jax.numpy as jnp
from jax import lax
from jax.experimental import pallas as pl
from jax.experimental.pallas import tpu as pltpu
from jax.sharding import Mesh
from jax.sharding import PartitionSpec as P

HEAD_DIM = 32
BLOCK = 128
BLK_DEV = 4
GROUP = 2
UNROLL = 8
EMPTY = 64
STAGES = ((0, 8), (8, 16), (24, 8))
NN = (((1,), (0,)), ((), ()))
NT = (((1,), (1,)), ((), ()))
TN = (((0,), (0,)), ((), ()))
TT = (((0,), (1,)), ((), ()))
F32 = jnp.float32
BF16 = jnp.bfloat16
EXP2_SCALE = math.log2(math.e) / math.sqrt(HEAD_DIM)


def dot(a, b, dims):
    return lax.dot_general(a, b, dims, preferred_element_type=F32)


def full(shape):
    return pl.BlockSpec(shape, lambda *_: (0,) * len(shape))


def call(kernel, outs, args, name, scalars=(), scratch=(), flops=10**6, trans=0, after=()):
    moved = sum(a.size * a.dtype.itemsize for a in args)
    return pl.pallas_call(
        kernel,
        grid_spec=pltpu.PrefetchScalarGridSpec(
            num_scalar_prefetch=len(scalars),
            grid=(1,),
            in_specs=[full(a.shape) for a in args] + [pl.BlockSpec(memory_space=pl.ANY)] * len(after),
            out_specs=[full(o.shape) for o in outs],
            scratch_shapes=list(scratch),
        ),
        out_shape=outs,
        compiler_params=pltpu.CompilerParams(vmem_limit_bytes=48 << 20),
        cost_estimate=pl.CostEstimate(flops=flops, bytes_accessed=moved, transcendentals=trans),
        name=name,
    )(*scalars, *args, *after)


def whole_rows(side_ref, own_ref, other_ref):
    own, other = own_ref[...], other_ref[...]
    first = side_ref[0] == 0
    return jnp.concatenate([jnp.where(first, own, other), jnp.where(first, other, own)], axis=1)


def prepare_kernel(place_ref, cells_ref, wk_ref, wv_ref, wq_ref, blocks_ref, partial_ref, rest_ref, codes_ref):
    side, zh, core = place_ref[0], place_ref[1], place_ref[2]
    mine = pl.ds(pl.multiple_of(side * BLOCK, BLOCK), BLOCK)
    theirs = pl.ds(pl.multiple_of((1 - side) * BLOCK, BLOCK), BLOCK)
    for n, w_ref in enumerate((wk_ref, wv_ref, wq_ref)):
        partial_ref[n] = dot(w_ref[mine, :], cells_ref[...], TT)
        rest_ref[n] = jnp.transpose(w_ref[theirs, :].astype(F32)).astype(BF16)

    def facts(ids):
        owner = ids // BLK_DEV
        far = (owner // 32 - zh) & 3
        stage = jnp.where(far == 0, 0, jnp.where(far == 2, 2, 1))
        mate = jnp.where(stage == 1, 8, 4)
        slot = jnp.where(owner % 2 != core, mate, 0) + owner // 2 % 4 + jnp.where(far == 1, 4, 0)
        return owner // 8 % 4, stage, slot * BLK_DEV + ids % BLK_DEV

    lane = lax.broadcasted_iota(jnp.int32, (32, 32), 1)
    below = lane < lax.broadcasted_iota(jnp.int32, (32, 32), 0)
    found = [[] for _ in range(4)]
    tally = [jnp.zeros((1, 32), F32) for _ in range(4)]
    for block in range(BLK_DEV):
        across = jnp.broadcast_to(blocks_ref[block : block + 1, :], (32, 32))
        down = jnp.transpose(across.astype(F32)).astype(jnp.int32)
        y_across, stage_across, _ = facts(across)
        y_down, stage_down, code = facts(down)
        same = (y_across == y_down) & (stage_across == stage_down) & below
        rank = jnp.sum(same.astype(F32), axis=1, keepdims=True).astype(jnp.int32)
        start = jnp.where(stage_down == 0, 0, jnp.where(stage_down == 1, 8, 24))
        at = rank + start == lane
        for y in range(4):
            row = jnp.sum(jnp.where(at & (y_down == y), code - EMPTY, 0).astype(F32), axis=0, keepdims=True)
            found[y].append(row + EMPTY)
            listed = (y_down == y) & (stage_down + 4 * block == lane)
            tally[y] = tally[y] + jnp.sum(listed.astype(F32), axis=0, keepdims=True)
    rows = []
    for y in range(4):
        units = jnp.maximum((tally[y].astype(jnp.int32) + GROUP - 1) // GROUP, 1).astype(F32)
        rows += [jnp.concatenate(found[y], axis=1), jnp.concatenate([units, jnp.zeros((1, 96), F32)], axis=1)]
    codes_ref[...] = jnp.concatenate(rows + [jnp.zeros((8, BLOCK), F32)], axis=0).astype(BF16)


def keyval_kernel(place_ref, partial_ref, rest_ref, other_ref, own_ref, *outs):
    *sends, keyval = outs
    other = other_ref[...]
    for n in range(2):
        flat = (partial_ref[n] + dot(rest_ref[n], other, NT)).astype(BF16)
        for head in range(4):
            ahead = (head - place_ref[3]) & 3
            for b in range(BLK_DEV):
                part = flat[head * 32 : head * 32 + 32, b * BLOCK : (b + 1) * BLOCK]
                keyval[ahead, n * BLOCK + b * 32 : n * BLOCK + b * 32 + 32, :] = part
    own_ref[...] = keyval[0]
    for d, ref in enumerate(sends):
        ref[...] = keyval[d + 1]


def query_kernel(partial_ref, rest_ref, other_ref, codes_ref, got0_ref, got1_ref, got2_ref, out_ref):
    flat = (partial_ref[2] + dot(rest_ref[2], other_ref[...], NT)).astype(BF16)
    for head in range(4):
        for y in range(4):
            for b in range(BLK_DEV):
                part = flat[head * 32 : head * 32 + 32, b * BLOCK : (b + 1) * BLOCK]
                out_ref[y * 4 + head, b * 32 : b * 32 + 32, :] = part
            out_ref[y * 4 + head, BLOCK : BLOCK + 16, :] = codes_ref[...]


def gather_kernel(place_ref, own_ref, *refs):
    *got, out_ref = refs
    for d, ref in enumerate((own_ref, *got)):
        out_ref[(place_ref[3] - d) & 3] = ref[...]


def relay_kernel(left_ref, right_ref, after_ref, low_ref, high_ref, both_ref):
    low_ref[...] = left_ref[:2]
    high_ref[...] = right_ref[2:]
    both_ref[:4] = left_ref[...]
    both_ref[4:] = right_ref[...]


def pass_kernel(low_ref, high_ref, after_ref, out_ref):
    out_ref[:2] = low_ref[...]
    out_ref[2:] = high_ref[...]


def source_kernel(side_ref, own_ref, other_ref, ws_ref, wt_ref, bias_ref, after_ref, source_ref, target_ref):
    whole = whole_rows(side_ref, own_ref, other_ref)
    for g in range(2):
        cols = slice(g * BLOCK, (g + 1) * BLOCK)
        source_ref[:, cols] = dot(whole, ws_ref[g], NN).astype(BF16)
        target_ref[:, cols] = dot(whole, wt_ref[g], NN) + bias_ref[g : g + 1, :]


def edge_kernel(wb_ref, before_ref, own_ref, after_ref, target_ref, edge_ref, cells_ref, out_ref, win):
    for side, ref in enumerate((before_ref, own_ref, after_ref)):
        for block in range(BLK_DEV):
            win[side * BLK_DEV + block] = ref[block * BLOCK : (block + 1) * BLOCK, :]
    lane = lax.broadcasted_iota(jnp.int32, (BLOCK, 4 * BLOCK), 1)

    def one(block, unused):
        rows = pl.ds(pl.multiple_of(block * BLOCK, BLOCK), BLOCK)
        table = jnp.concatenate([win[wb_ref[block, k]] for k in range(4)], axis=0)
        target = target_ref[rows, :]
        picks = edge_ref[rows, :]
        total = jnp.zeros((BLOCK, BLOCK), F32)
        for e in range(8):
            hot = (picks[:, e : e + 1] == lane).astype(F32).astype(BF16)
            pre = dot(hot, table, NN) + target
            gate = 0.5 + 0.5 * jnp.tanh(0.5 * pre[:, :BLOCK])
            value = pre[:, BLOCK:]
            total = total + gate * (value * (0.5 + 0.5 * jnp.tanh(0.5 * value)))
        out_ref[rows, :] = cells_ref[rows, :].astype(F32) + total * 0.125
        return unused

    lax.fori_loop(0, BLK_DEV, one, 0)


def load_blocks(pieces, keys, values):
    first = 0
    for ref in pieces:
        for x in range(ref.shape[0]):
            for b in range(BLK_DEV):
                part = ref[x, b * 32 : (b + 1) * 32, :].astype(F32)
                keys[first] = jnp.transpose(part).astype(BF16)
                values[first, 0:32, :] = ref[x, BLOCK + b * 32 : BLOCK + (b + 1) * 32, :]
                values[first, 32:48, :] = jnp.ones((16, BLOCK), BF16)
                first += 1
    keys[first] = jnp.zeros((BLOCK, 32), BF16)
    values[first] = jnp.zeros((48, BLOCK), BF16)


def accumulate(stage, unroll, list_ref, start, end, queries, keys, values, acc, scored):
    base = STAGES[stage][0]
    spare = keys.shape[0] - 1

    def length(i):
        return list_ref[(i >> 2) * 2 + 1, ((i & 3) << 2) + stage]

    def following(i, j):
        over = j + 1 >= length(i)
        return jnp.where(over, jnp.minimum(i + 1, end), i), jnp.where(over, 0, j + 1)

    def batch(i, j):
        units = [(i, j)]
        for _ in range(unroll - 1):
            units.append(following(*units[-1]))
        return units

    def picked(table, axis, i, j):
        row, column = (i >> 2) * 2, ((i & 3) << 5) + base + j * GROUP
        blocks = [jnp.where(i < end, jnp.minimum(list_ref[row, column + g], spare), spare) for g in range(GROUP)]
        return jnp.concatenate([table[block] for block in blocks], axis=axis)

    def scores(units):
        for w, (i, j) in enumerate(units):
            scored[w] = dot(picked(keys, 0, i, j), queries[i - start], NN)

    def step(u, state):
        now = [(state[2 * w], state[2 * w + 1]) for w in range(unroll)]
        later = batch(*following(*now[-1]))
        weights = [jnp.exp2(scored[w] * EXP2_SCALE).astype(BF16) for w in range(unroll)]
        scores(later)
        for w, (i, j) in enumerate(now):
            acc[i - start] = acc[i - start] + dot(picked(values, 1, i, j), weights[w], NN)[0:40, :]
        return tuple(v for pair in later for v in pair)

    count = lax.fori_loop(start, end, lambda i, s: s + length(i), jnp.int32(0))
    begin = batch(jnp.int32(0) + start, jnp.int32(0))
    scores(begin)
    lax.fori_loop(0, (count + unroll - 1) // unroll, step, tuple(v for pair in begin for v in pair))


def attend_kernel(stage, npieces, resume, list_ref, q_ref, *refs):
    last = stage == len(STAGES) - 1
    pieces, refs = refs[:npieces], refs[npieces:]
    out_ref, queries, keys, values, scored, *rest = refs[1:] if resume else refs
    acc = rest[0] if last else out_ref
    for m in range(64):
        top = (m % 4) * 32
        queries[m] = q_ref[m // 16, m // 4 % 4, top : top + 32, :]
    queries[64] = jnp.zeros((32, BLOCK), BF16)
    load_blocks(pieces, keys, values)
    acc[...] = refs[0][...] if resume else jnp.zeros(acc.shape, F32)
    accumulate(stage, UNROLL, list_ref, 0, 64, queries, keys, values, acc, scored)
    if last:
        for y in range(4):
            for m in range(16):
                a = acc[y * 16 + m]
                out_ref[y, m * 32 : (m + 1) * 32, :] = a[0:32, :]
                out_ref[y, 512 + m : 513 + m, :] = a[32:33, :]


def attend(stage, lists, q_all, pieces, carry, flops):
    last = stage == len(STAGES) - 1
    blocks = STAGES[stage][1] * BLK_DEV + 1
    scratch = [
        pltpu.VMEM((65, 32, BLOCK), BF16),
        pltpu.VMEM((blocks, BLOCK, 32), BF16),
        pltpu.VMEM((blocks, 48, BLOCK), BF16),
        pltpu.VMEM((UNROLL, BLOCK * GROUP, BLOCK), F32),
    ]
    if last:
        scratch.append(pltpu.VMEM((65, 40, BLOCK), F32))
    (out,) = call(
        functools.partial(attend_kernel, stage, len(pieces), carry is not None),
        [shaped((4, 528, BLOCK) if last else (65, 40, BLOCK), F32)],
        [q_all, *pieces] + ([] if carry is None else [carry]),
        "attend" + str(stage),
        scalars=(lists,),
        scratch=scratch,
        flops=flops,
    )
    return out


def mix_kernel(part_ref, weight_ref, out_ref):
    total = part_ref[0] + part_ref[1] + part_ref[2] + part_ref[3]
    for m in range(16):
        mixed = (total[m * 32 : (m + 1) * 32, :] / total[512 + m : 513 + m, :]).astype(BF16)
        for peer in range(2):
            out_ref[(m // 4) * 2 + peer, (m % 4) * 32 : (m % 4) * 32 + 32, :] = mixed


def final_kernel(place_ref, mixed_ref, w_mine_ref, w_other_ref, base_ref, out_ref):
    side = place_ref[0]
    columns = pl.ds(pl.multiple_of(side * BLOCK, BLOCK), BLOCK)
    mine, other = w_mine_ref[:, columns], w_other_ref[:, columns]
    halves = (jnp.where(side == 0, mine, other), jnp.where(side == 0, other, mine))
    weight = jnp.concatenate([h[x * 32 : x * 32 + 32, :] for x in range(4) for h in halves], axis=0)
    for block in range(BLK_DEV):
        rows = slice(block * BLOCK, (block + 1) * BLOCK)
        mixed = jnp.concatenate([mixed_ref[k, block * 32 : block * 32 + 32, :] for k in range(8)], axis=0)
        out_ref[rows, :] = (base_ref[rows, :] + dot(mixed, weight, TN)).astype(BF16)


def shaped(shape, dtype):
    return jax.ShapeDtypeStruct(shape, dtype)


def body(cells, w_query, w_key, w_value, w_source, w_target, msg_bias, w_out, nbr_block, edge_src, key_blocks):
    rows = cells.shape[0]
    everyone = ("zh", "y", "x", "c")
    nparts = 128
    mine = lax.axis_index(everyone)
    side = lax.axis_index("h")
    swap = [(0, 1), (1, 0)]
    ring = [[(i, (i + d) % 4) for i in range(4)] for d in range(4)]
    other = lax.ppermute(cells, "h", swap)
    w_got = lax.ppermute(w_out, "h", swap)
    sides = side.reshape(1)
    places = jnp.stack([side, lax.axis_index("zh"), lax.axis_index("c"), lax.axis_index("x")])
    partial, rest, codes = call(
        prepare_kernel,
        [shaped((3, BLOCK, rows), F32), shaped((3, BLOCK, BLOCK), BF16), shaped((16, BLOCK), BF16)],
        [cells, w_key, w_value, w_query, key_blocks],
        "prepare",
        scalars=(places,),
    )
    own, *sends = call(
        keyval_kernel,
        [shaped((256, BLOCK), BF16)] * 4,
        [partial, rest, other],
        "keyval",
        scalars=(places,),
        scratch=[pltpu.VMEM((4, 256, BLOCK), BF16)],
    )
    got = [lax.ppermute(v, "x", ring[d + 1]) for d, v in enumerate(sends)]
    (here,) = call(gather_kernel, [shaped((4, 256, BLOCK), BF16)], [own, *got], "gather", scalars=(places,))
    left = lax.ppermute(here, "zh", ring[1])
    right = lax.ppermute(here, "zh", ring[3])
    mate_here = lax.ppermute(here, "c", swap)
    (query,) = call(
        query_kernel, [shaped((16, 144, BLOCK), BF16)], [partial, rest, other, codes], "query", after=got
    )
    q_all = lax.all_to_all(query, ("y", "x"), 0, 0).reshape(4, 4, 144, BLOCK)
    lists = lax.dynamic_slice_in_dim(q_all, BLOCK + 2 * lax.axis_index("y"), 2, 2)
    lists = jnp.pad(lists.reshape(32, BLOCK).astype(jnp.int32), ((0, 8), (0, 0)), constant_values=EMPTY)
    partial = attend(0, lists, q_all, [here, mate_here], None, 10**6)
    shapes = [shaped((n, 256, BLOCK), BF16) for n in (2, 2, 8)]
    low, high, both = call(relay_kernel, shapes, [left, right], "relay", after=[partial])
    far_low = lax.ppermute(low, "zh", ring[1])
    far_high = lax.ppermute(high, "zh", ring[3])
    partial = attend(1, lists, q_all, [both, lax.ppermute(both, "c", swap)], partial, 9 * 10**9)
    (across,) = call(pass_kernel, [shaped((4, 256, BLOCK), BF16)], [far_low, far_high], "across", after=[partial])
    partial = attend(2, lists, q_all, [across, lax.ppermute(across, "c", swap)], partial, 5 * 10**9)
    source, target = call(
        source_kernel,
        [shaped((rows, 256), BF16), shaped((rows, 256), F32)],
        [cells, other, w_source, w_target, msg_bias],
        "source",
        scalars=(sides,),
        after=[partial],
    )
    up = [(i, (i + 1) % nparts) for i in range(nparts)]
    before = lax.ppermute(source, everyone, up)
    after = lax.ppermute(source, everyone, [(j, i) for i, j in up])
    window_block = (nbr_block // BLK_DEV - mine + 1) % nparts * BLK_DEV + nbr_block % BLK_DEV
    (base,) = call(
        edge_kernel,
        [shaped((rows, BLOCK), F32)],
        [before, source, after, target, edge_src, cells],
        "edge",
        scalars=(window_block,),
        scratch=[pltpu.VMEM((12, BLOCK, 256), BF16)],
        flops=3 * 10**9,
        trans=10**6,
    )
    (mixed,) = call(mix_kernel, [shaped((8, BLOCK, BLOCK), BF16)], [lax.all_to_all(partial, "y", 0, 0)], "mix", after=[w_got])
    mixed = lax.all_to_all(mixed, ("x", "h"), 0, 0)
    (out,) = call(
        final_kernel, [shaped((rows, BLOCK), BF16)], [mixed, w_out, w_got, base], "final", scalars=(places,)
    )
    return out


def solution(mesh):
    split = Mesh(mesh.devices.reshape(4, 4, 4, 2, 2), ("zh", "y", "x", "c", "h"))
    blk = ("zh", "y", "x", "c")
    in_specs = (
        P(blk, "h"),
        P(None, "h"),
        P(None, "h"),
        P(None, "h"),
        P(None, None, "h"),
        P(None, None, "h"),
        P(None, "h"),
        P("h", None),
        P(blk, None),
        P(blk, None),
        P(blk, None),
    )
    return jax.shard_map(body, mesh=split, in_specs=in_specs, out_specs=P(blk, "h"), check_vma=False)
```

```python
import functools
import math

import jax
import jax.numpy as jnp
from jax import lax
from jax.experimental import pallas as pl
from jax.experimental.pallas import tpu as pltpu
from jax.sharding import Mesh
from jax.sharding import PartitionSpec as P

HEAD_DIM = 32
BLOCK = 128
BLK_DEV = 4
GROUP = 2
UNROLL = 8
EMPTY = 64
STAGES = ((0, 8), (8, 16), (24, 8))
NN = (((1,), (0,)), ((), ()))
NT = (((1,), (1,)), ((), ()))
TN = (((0,), (0,)), ((), ()))
TT = (((0,), (1,)), ((), ()))
F32 = jnp.float32
BF16 = jnp.bfloat16
EXP2_SCALE = math.log2(math.e) / math.sqrt(HEAD_DIM)


def dot(a, b, dims):
    return lax.dot_general(a, b, dims, preferred_element_type=F32)


def full(shape):
    return pl.BlockSpec(shape, lambda *_: (0,) * len(shape))


def call(kernel, outs, args, name, scalars=(), scratch=(), flops=10**6, trans=0, after=()):
    moved = sum(a.size * a.dtype.itemsize for a in args)
    return pl.pallas_call(
        kernel,
        grid_spec=pltpu.PrefetchScalarGridSpec(
            num_scalar_prefetch=len(scalars),
            grid=(1,),
            in_specs=[full(a.shape) for a in args] + [pl.BlockSpec(memory_space=pl.ANY)] * len(after),
            out_specs=[full(o.shape) for o in outs],
            scratch_shapes=list(scratch),
        ),
        out_shape=outs,
        compiler_params=pltpu.CompilerParams(vmem_limit_bytes=48 << 20),
        cost_estimate=pl.CostEstimate(flops=flops, bytes_accessed=moved, transcendentals=trans),
        name=name,
    )(*scalars, *args, *after)


def whole_rows(side, own, other):
    first = side == 0
    return jnp.concatenate([jnp.where(first, own, other), jnp.where(first, other, own)], axis=1)


def prepare_kernel(place_ref, cells_ref, wk_ref, wv_ref, wq_ref, blocks_ref, partial_ref, rest_ref, codes_ref):
    side, zh, core = place_ref[0], place_ref[1], place_ref[2]
    mine = pl.ds(pl.multiple_of(side * BLOCK, BLOCK), BLOCK)
    theirs = pl.ds(pl.multiple_of((1 - side) * BLOCK, BLOCK), BLOCK)
    for n, w_ref in enumerate((wk_ref, wv_ref, wq_ref)):
        partial_ref[n] = dot(w_ref[mine, :], cells_ref[...], TT)
        rest_ref[n] = jnp.transpose(w_ref[theirs, :].astype(F32)).astype(BF16)

    def facts(ids):
        owner = ids // BLK_DEV
        far = (owner // 32 - zh) & 3
        stage = jnp.where(far == 0, 0, jnp.where(far == 2, 2, 1))
        mate = jnp.where(stage == 1, 8, 4)
        slot = jnp.where(owner % 2 != core, mate, 0) + owner // 2 % 4 + jnp.where(far == 1, 4, 0)
        return owner // 8 % 4, stage, slot * BLK_DEV + ids % BLK_DEV

    lane = lax.broadcasted_iota(jnp.int32, (32, 32), 1)
    below = lane < lax.broadcasted_iota(jnp.int32, (32, 32), 0)
    found = [[] for _ in range(4)]
    tally = [jnp.zeros((1, 32), F32) for _ in range(4)]
    for block in range(BLK_DEV):
        across = jnp.broadcast_to(blocks_ref[block : block + 1, :], (32, 32))
        down = jnp.transpose(across.astype(F32)).astype(jnp.int32)
        y_across, stage_across, _ = facts(across)
        y_down, stage_down, code = facts(down)
        same = (y_across == y_down) & (stage_across == stage_down) & below
        rank = jnp.sum(same.astype(F32), axis=1, keepdims=True).astype(jnp.int32)
        start = jnp.where(stage_down == 0, 0, jnp.where(stage_down == 1, 8, 24))
        at = rank + start == lane
        for y in range(4):
            row = jnp.sum(jnp.where(at & (y_down == y), code - EMPTY, 0).astype(F32), axis=0, keepdims=True)
            found[y].append(row + EMPTY)
            listed = (y_down == y) & (stage_down + 4 * block == lane)
            tally[y] = tally[y] + jnp.sum(listed.astype(F32), axis=0, keepdims=True)
    rows = []
    for y in range(4):
        units = jnp.maximum((tally[y].astype(jnp.int32) + GROUP - 1) // GROUP, 1).astype(F32)
        rows += [jnp.concatenate(found[y], axis=1), jnp.concatenate([units, jnp.zeros((1, 96), F32)], axis=1)]
    codes_ref[...] = jnp.concatenate(rows + [jnp.zeros((8, BLOCK), F32)], axis=0).astype(BF16)


def keyval_kernel(place_ref, partial_ref, rest_ref, other_ref, up_ref, down_ref, own_ref, *outs):
    *sends, keyval = outs
    other = other_ref[...]
    for n in range(2):
        flat = (partial_ref[n] + dot(rest_ref[n], other, NT)).astype(BF16)
        for head in range(4):
            ahead = (head - place_ref[3]) & 3
            for b in range(BLK_DEV):
                part = flat[head * 32 : head * 32 + 32, b * BLOCK : (b + 1) * BLOCK]
                keyval[ahead, n * BLOCK + b * 32 : n * BLOCK + b * 32 + 32, :] = part
    own_ref[...] = keyval[0]
    for d, ref in enumerate(sends):
        ref[...] = keyval[d + 1]


def query_kernel(partial_ref, rest_ref, other_ref, codes_ref, got0_ref, got1_ref, got2_ref, out_ref):
    flat = (partial_ref[2] + dot(rest_ref[2], other_ref[...], NT)).astype(BF16)
    for head in range(4):
        for y in range(4):
            for b in range(BLK_DEV):
                part = flat[head * 32 : head * 32 + 32, b * BLOCK : (b + 1) * BLOCK]
                out_ref[y * 4 + head, b * 32 : b * 32 + 32, :] = part
            out_ref[y * 4 + head, BLOCK : BLOCK + 16, :] = codes_ref[...]


def gather_kernel(place_ref, own_ref, *refs):
    *got, out_ref = refs
    for d, ref in enumerate((own_ref, *got)):
        out_ref[(place_ref[3] - d) & 3] = ref[...]


def relay_kernel(left_ref, right_ref, after_ref, low_ref, high_ref, both_ref):
    low_ref[...] = left_ref[:2]
    high_ref[...] = right_ref[2:]
    both_ref[:4] = left_ref[...]
    both_ref[4:] = right_ref[...]


def pass_kernel(low_ref, high_ref, after_ref, out_ref):
    out_ref[:2] = low_ref[...]
    out_ref[2:] = high_ref[...]


def ends_kernel(place_ref, cells_ref, up_ref, down_ref, wait_ref, before_ref, after_ref):
    spot = place_ref[4] * 8 + place_ref[3] * 2 + place_ref[2]
    cells = cells_ref[...]
    before_ref[...] = jnp.where(spot == 31, up_ref[...], cells)
    after_ref[...] = jnp.where(spot == 0, down_ref[...], cells)


def pair_kernel(before_ref, after_ref, out_ref):
    rows = before_ref.shape[0]
    out_ref[:rows, :] = before_ref[...]
    out_ref[rows:, :] = after_ref[...]


def edge_kernel(
    wb_ref, place_ref, own_ref, other_ref, near_ref, near_other_ref, ws_ref, wt_ref, bias_ref, edge_ref, out_ref, win, tgt
):
    side = place_ref[0]
    rows = own_ref.shape[0]
    whole = whole_rows(side, own_ref[...], other_ref[...])
    for g in range(2):
        tgt[:, g * BLOCK : (g + 1) * BLOCK] = dot(whole, wt_ref[g], NN) + bias_ref[g : g + 1, :]
    for spot, cells in enumerate(
        (
            whole_rows(side, near_ref[:rows, :], near_other_ref[:rows, :]),
            whole,
            whole_rows(side, near_ref[rows:, :], near_other_ref[rows:, :]),
        )
    ):
        for g in range(2):
            source = dot(cells, ws_ref[g], NN).astype(BF16)
            for block in range(BLK_DEV):
                win[spot * BLK_DEV + block, :, g * BLOCK : (g + 1) * BLOCK] = source[block * BLOCK : (block + 1) * BLOCK, :]
    lane = lax.broadcasted_iota(jnp.int32, (BLOCK, 4 * BLOCK), 1)

    def one(block, unused):
        rows = pl.ds(pl.multiple_of(block * BLOCK, BLOCK), BLOCK)
        table = jnp.concatenate([win[wb_ref[block, k]] for k in range(4)], axis=0)
        target = tgt[rows, :]
        picks = edge_ref[rows, :]
        total = jnp.zeros((BLOCK, BLOCK), F32)
        for e in range(8):
            hot = (picks[:, e : e + 1] == lane).astype(F32).astype(BF16)
            pre = dot(hot, table, NN) + target
            gate = 0.5 + 0.5 * jnp.tanh(0.5 * pre[:, :BLOCK])
            value = pre[:, BLOCK:]
            total = total + gate * (value * (0.5 + 0.5 * jnp.tanh(0.5 * value)))
        out_ref[rows, :] = own_ref[rows, :].astype(F32) + total * 0.125
        return unused

    lax.fori_loop(0, BLK_DEV, one, 0)


def load_blocks(pieces, keys, values):
    first = 0
    for ref in pieces:
        for x in range(ref.shape[0]):
            for b in range(BLK_DEV):
                part = ref[x, b * 32 : (b + 1) * 32, :].astype(F32)
                keys[first] = jnp.transpose(part).astype(BF16)
                values[first, 0:32, :] = ref[x, BLOCK + b * 32 : BLOCK + (b + 1) * 32, :]
                values[first, 32:48, :] = jnp.ones((16, BLOCK), BF16)
                first += 1
    keys[first] = jnp.zeros((BLOCK, 32), BF16)
    values[first] = jnp.zeros((48, BLOCK), BF16)


def accumulate(stage, unroll, list_ref, start, end, queries, keys, values, acc, scored):
    base = STAGES[stage][0]
    spare = keys.shape[0] - 1

    def length(i):
        return list_ref[(i >> 2) * 2 + 1, ((i & 3) << 2) + stage]

    def following(i, j):
        over = j + 1 >= length(i)
        return jnp.where(over, jnp.minimum(i + 1, end), i), jnp.where(over, 0, j + 1)

    def batch(i, j):
        units = [(i, j)]
        for _ in range(unroll - 1):
            units.append(following(*units[-1]))
        return units

    def picked(table, axis, i, j):
        row, column = (i >> 2) * 2, ((i & 3) << 5) + base + j * GROUP
        blocks = [jnp.where(i < end, jnp.minimum(list_ref[row, column + g], spare), spare) for g in range(GROUP)]
        return jnp.concatenate([table[block] for block in blocks], axis=axis)

    def scores(units):
        for w, (i, j) in enumerate(units):
            scored[w] = dot(picked(keys, 0, i, j), queries[i - start], NN)

    def step(u, state):
        now = [(state[2 * w], state[2 * w + 1]) for w in range(unroll)]
        later = batch(*following(*now[-1]))
        weights = [jnp.exp2(scored[w] * EXP2_SCALE).astype(BF16) for w in range(unroll)]
        scores(later)
        for w, (i, j) in enumerate(now):
            acc[i - start] = acc[i - start] + dot(picked(values, 1, i, j), weights[w], NN)[0:40, :]
        return tuple(v for pair in later for v in pair)

    count = lax.fori_loop(start, end, lambda i, s: s + length(i), jnp.int32(0))
    begin = batch(jnp.int32(0) + start, jnp.int32(0))
    scores(begin)
    lax.fori_loop(0, (count + unroll - 1) // unroll, step, tuple(v for pair in begin for v in pair))


def attend_kernel(stage, npieces, resume, list_ref, q_ref, *refs):
    last = stage == len(STAGES) - 1
    pieces, refs = refs[:npieces], refs[npieces:]
    out_ref, queries, keys, values, scored, *rest = refs[1:] if resume else refs
    acc = rest[0] if last else out_ref
    for m in range(64):
        top = (m % 4) * 32
        queries[m] = q_ref[m // 16, m // 4 % 4, top : top + 32, :]
    queries[64] = jnp.zeros((32, BLOCK), BF16)
    load_blocks(pieces, keys, values)
    acc[...] = refs[0][...] if resume else jnp.zeros(acc.shape, F32)
    accumulate(stage, UNROLL, list_ref, 0, 64, queries, keys, values, acc, scored)
    if last:
        for y in range(4):
            for m in range(16):
                a = acc[y * 16 + m]
                out_ref[y, m * 32 : (m + 1) * 32, :] = a[0:32, :]
                out_ref[y, 512 + m : 513 + m, :] = a[32:33, :]


def attend(stage, lists, q_all, pieces, carry, flops):
    last = stage == len(STAGES) - 1
    blocks = STAGES[stage][1] * BLK_DEV + 1
    scratch = [
        pltpu.VMEM((65, 32, BLOCK), BF16),
        pltpu.VMEM((blocks, BLOCK, 32), BF16),
        pltpu.VMEM((blocks, 48, BLOCK), BF16),
        pltpu.VMEM((UNROLL, BLOCK * GROUP, BLOCK), F32),
    ]
    if last:
        scratch.append(pltpu.VMEM((65, 40, BLOCK), F32))
    (out,) = call(
        functools.partial(attend_kernel, stage, len(pieces), carry is not None),
        [shaped((4, 528, BLOCK) if last else (65, 40, BLOCK), F32)],
        [q_all, *pieces] + ([] if carry is None else [carry]),
        "attend" + str(stage),
        scalars=(lists,),
        scratch=scratch,
        flops=flops,
    )
    return out


def mix_kernel(part_ref, weight_ref, out_ref):
    total = part_ref[0] + part_ref[1] + part_ref[2] + part_ref[3]
    for m in range(16):
        mixed = (total[m * 32 : (m + 1) * 32, :] / total[512 + m : 513 + m, :]).astype(BF16)
        for peer in range(2):
            out_ref[(m // 4) * 2 + peer, (m % 4) * 32 : (m % 4) * 32 + 32, :] = mixed


def weight_kernel(place_ref, w_mine_ref, w_other_ref, out_ref):
    side = place_ref[0]
    columns = pl.ds(pl.multiple_of(side * BLOCK, BLOCK), BLOCK)
    mine, other = w_mine_ref[:, columns], w_other_ref[:, columns]
    halves = (jnp.where(side == 0, mine, other), jnp.where(side == 0, other, mine))
    out_ref[...] = jnp.concatenate([h[x * 32 : x * 32 + 32, :] for x in range(4) for h in halves], axis=0)


def final_kernel(mixed_ref, weight_ref, base_ref, out_ref):
    for block in range(BLK_DEV):
        rows = slice(block * BLOCK, (block + 1) * BLOCK)
        mixed = jnp.concatenate([mixed_ref[k, block * 32 : block * 32 + 32, :] for k in range(8)], axis=0)
        out_ref[rows, :] = (base_ref[rows, :] + dot(mixed, weight_ref[...], TN)).astype(BF16)


def shaped(shape, dtype):
    return jax.ShapeDtypeStruct(shape, dtype)


def body(cells, w_query, w_key, w_value, w_source, w_target, msg_bias, w_out, nbr_block, edge_src, key_blocks):
    rows = cells.shape[0]
    everyone = ("zh", "y", "x", "c")
    nparts = 128
    mine = lax.axis_index(everyone)
    side = lax.axis_index("h")
    swap = [(0, 1), (1, 0)]
    ring = [[(i, (i + d) % 4) for i in range(4)] for d in range(4)]
    other = lax.ppermute(cells, "h", swap)
    w_got = lax.ppermute(w_out, "h", swap)
    tops = [(z * 32 + 31, (z + 1) % 4 * 32 + 31) for z in range(4)]
    bottoms = [((z + 1) % 4 * 32, z * 32) for z in range(4)]
    up = lax.ppermute(cells, everyone, tops)
    down = lax.ppermute(cells, everyone, bottoms)
    places = jnp.stack([side, lax.axis_index("zh"), lax.axis_index("c"), lax.axis_index("x"), lax.axis_index("y")])
    partial, rest, codes = call(
        prepare_kernel,
        [shaped((3, BLOCK, rows), F32), shaped((3, BLOCK, BLOCK), BF16), shaped((16, BLOCK), BF16)],
        [cells, w_key, w_value, w_query, key_blocks],
        "prepare",
        scalars=(places,),
    )
    own, *sends = call(
        keyval_kernel,
        [shaped((256, BLOCK), BF16)] * 4,
        [partial, rest, other],
        "keyval",
        scalars=(places,),
        scratch=[pltpu.VMEM((4, 256, BLOCK), BF16)],
        after=[up, down],
    )
    got = [lax.ppermute(v, "x", ring[d + 1]) for d, v in enumerate(sends)]
    (here,) = call(gather_kernel, [shaped((4, 256, BLOCK), BF16)], [own, *got], "gather", scalars=(places,))
    left = lax.ppermute(here, "zh", ring[1])
    right = lax.ppermute(here, "zh", ring[3])
    mate_here = lax.ppermute(here, "c", swap)
    (query,) = call(
        query_kernel, [shaped((16, 144, BLOCK), BF16)], [partial, rest, other, codes], "query", after=got
    )
    q_all = lax.all_to_all(query, ("y", "x"), 0, 0).reshape(4, 4, 144, BLOCK)
    lists = lax.dynamic_slice_in_dim(q_all, BLOCK + 2 * lax.axis_index("y"), 2, 2)
    lists = jnp.pad(lists.reshape(32, BLOCK).astype(jnp.int32), ((0, 8), (0, 0)), constant_values=EMPTY)
    partial = attend(0, lists, q_all, [here, mate_here], None, 10**6)
    shapes = [shaped((n, 256, BLOCK), BF16) for n in (2, 2, 8)]
    low, high, both = call(relay_kernel, shapes, [left, right], "relay", after=[partial])
    far_low = lax.ppermute(low, "zh", ring[1])
    far_high = lax.ppermute(high, "zh", ring[3])
    partial = attend(1, lists, q_all, [both, lax.ppermute(both, "c", swap)], partial, 9 * 10**9)
    (across,) = call(pass_kernel, [shaped((4, 256, BLOCK), BF16)], [far_low, far_high], "across", after=[partial])
    partial = attend(2, lists, q_all, [across, lax.ppermute(across, "c", swap)], partial, 5 * 10**9)
    plane = [(i, (i + 1) % 32) for i in range(32)]
    ends = [shaped((rows, BLOCK), BF16)] * 2
    before, after = call(ends_kernel, ends, [cells, up, down], "ends", scalars=(places,), after=[partial])
    before = lax.ppermute(before, ("y", "x", "c"), plane)
    after = lax.ppermute(after, ("y", "x", "c"), [(j, i) for i, j in plane])
    (around,) = call(pair_kernel, [shaped((2 * rows, BLOCK), BF16)], [before, after], "around")
    around_other = lax.ppermute(around, "h", swap)
    window_block = (nbr_block // BLK_DEV - mine + 1) % nparts * BLK_DEV + nbr_block % BLK_DEV
    (base,) = call(
        edge_kernel,
        [shaped((rows, BLOCK), F32)],
        [cells, other, around, around_other, w_source, w_target, msg_bias, edge_src],
        "edge",
        scalars=(window_block, places),
        scratch=[pltpu.VMEM((12, BLOCK, 256), BF16), pltpu.VMEM((rows, 256), F32)],
        flops=4 * 10**9,
        trans=10**6,
    )
    (w_full,) = call(weight_kernel, [shaped((256, BLOCK), BF16)], [w_out, w_got], "weight", scalars=(places,))
    (mixed,) = call(mix_kernel, [shaped((8, BLOCK, BLOCK), BF16)], [lax.all_to_all(partial, "y", 0, 0)], "mix", after=[w_full])
    mixed = lax.all_to_all(mixed, ("x", "h"), 0, 0)
    (out,) = call(
        final_kernel, [shaped((rows, BLOCK), BF16)], [mixed, w_full, base], "final"
    )
    return out


def solution(mesh):
    split = Mesh(mesh.devices.reshape(4, 4, 4, 2, 2), ("zh", "y", "x", "c", "h"))
    blk = ("zh", "y", "x", "c")
    in_specs = (
        P(blk, "h"),
        P(None, "h"),
        P(None, "h"),
        P(None, "h"),
        P(None, None, "h"),
        P(None, None, "h"),
        P(None, "h"),
        P("h", None),
        P(blk, None),
        P(blk, None),
        P(blk, None),
    )
    return jax.shard_map(body, mesh=split, in_specs=in_specs, out_specs=P(blk, "h"), check_vma=False)
```

```python
import functools
import math

import jax
import jax.numpy as jnp
from jax import lax
from jax.experimental import pallas as pl
from jax.experimental.pallas import tpu as pltpu
from jax.sharding import Mesh
from jax.sharding import PartitionSpec as P

HEAD_DIM = 32
BLOCK = 128
BLK_DEV = 4
GROUP = 2
UNROLL = 8
EMPTY = 64
STAGES = ((0, 8), (8, 16), (24, 8))
NN = (((1,), (0,)), ((), ()))
NT = (((1,), (1,)), ((), ()))
TN = (((0,), (0,)), ((), ()))
TT = (((0,), (1,)), ((), ()))
F32 = jnp.float32
BF16 = jnp.bfloat16
EXP2_SCALE = math.log2(math.e) / math.sqrt(HEAD_DIM)


def dot(a, b, dims):
    return lax.dot_general(a, b, dims, preferred_element_type=F32)


def full(shape):
    return pl.BlockSpec(shape, lambda *_: (0,) * len(shape))


def call(kernel, outs, args, name, scalars=(), scratch=(), flops=10**6, trans=0, after=()):
    moved = sum(a.size * a.dtype.itemsize for a in args)
    return pl.pallas_call(
        kernel,
        grid_spec=pltpu.PrefetchScalarGridSpec(
            num_scalar_prefetch=len(scalars),
            grid=(1,),
            in_specs=[full(a.shape) for a in args] + [pl.BlockSpec(memory_space=pl.ANY)] * len(after),
            out_specs=[full(o.shape) for o in outs],
            scratch_shapes=list(scratch),
        ),
        out_shape=outs,
        compiler_params=pltpu.CompilerParams(vmem_limit_bytes=48 << 20),
        cost_estimate=pl.CostEstimate(flops=flops, bytes_accessed=moved, transcendentals=trans),
        name=name,
    )(*scalars, *args, *after)


def whole_rows(side, own, other):
    first = side == 0
    return jnp.concatenate([jnp.where(first, own, other), jnp.where(first, other, own)], axis=1)


def prepare_kernel(place_ref, cells_ref, weights_ref, blocks_ref, partial_ref, rest_ref, codes_ref):
    side, zh, core = place_ref[0], place_ref[1], place_ref[2]

    def facts(ids):
        owner = ids // BLK_DEV
        far = (owner // 32 - zh) & 3
        stage = jnp.where(far == 0, 0, jnp.where(far == 2, 2, 1))
        mate = jnp.where(stage == 1, 8, 4)
        slot = jnp.where(owner % 2 != core, mate, 0) + owner // 2 % 4 + jnp.where(far == 1, 4, 0)
        return owner // 8 % 4, stage, slot * BLK_DEV + ids % BLK_DEV

    lane = lax.broadcasted_iota(jnp.int32, (32, 32), 1)
    below = lane < lax.broadcasted_iota(jnp.int32, (32, 32), 0)
    found = [[] for _ in range(4)]
    tally = [jnp.zeros((1, 32), F32) for _ in range(4)]
    for block in range(BLK_DEV):
        across = jnp.broadcast_to(blocks_ref[block : block + 1, :], (32, 32))
        down = jnp.transpose(across.astype(F32)).astype(jnp.int32)
        y_across, stage_across, _ = facts(across)
        y_down, stage_down, code = facts(down)
        same = (y_across == y_down) & (stage_across == stage_down) & below
        rank = jnp.sum(same.astype(F32), axis=1, keepdims=True).astype(jnp.int32)
        start = jnp.where(stage_down == 0, 0, jnp.where(stage_down == 1, 8, 24))
        at = rank + start == lane
        for y in range(4):
            row = jnp.sum(jnp.where(at & (y_down == y), code - EMPTY, 0).astype(F32), axis=0, keepdims=True)
            found[y].append(row + EMPTY)
            listed = (y_down == y) & (stage_down + 4 * block == lane)
            tally[y] = tally[y] + jnp.sum(listed.astype(F32), axis=0, keepdims=True)
    rows = []
    for y in range(4):
        units = jnp.maximum((tally[y].astype(jnp.int32) + GROUP - 1) // GROUP, 1).astype(F32)
        rows += [jnp.concatenate(found[y], axis=1), jnp.concatenate([units, jnp.zeros((1, 96), F32)], axis=1)]
    codes_ref[...] = jnp.concatenate(rows + [jnp.zeros((8, BLOCK), F32)], axis=0).astype(BF16)
    mine = pl.ds(pl.multiple_of(side * BLOCK, BLOCK), BLOCK)
    theirs = pl.ds(pl.multiple_of((1 - side) * BLOCK, BLOCK), BLOCK)
    for n in range(3):
        partial_ref[n] = dot(weights_ref[n, mine, :], cells_ref[...], TT)
        rest_ref[n] = jnp.transpose(weights_ref[n, theirs, :].astype(F32)).astype(BF16)


def keyval_kernel(place_ref, partial_ref, rest_ref, other_ref, own_ref, *outs):
    *sends, keyval = outs
    other = other_ref[...]
    for n in range(2):
        flat = (partial_ref[n] + dot(rest_ref[n], other, NT)).astype(BF16)
        for head in range(4):
            ahead = (head - place_ref[3]) & 3
            for b in range(BLK_DEV):
                part = flat[head * 32 : head * 32 + 32, b * BLOCK : (b + 1) * BLOCK]
                keyval[ahead, n * BLOCK + b * 32 : n * BLOCK + b * 32 + 32, :] = part
    own_ref[...] = keyval[0]
    for d, ref in enumerate(sends):
        ref[...] = keyval[d + 1]


def query_kernel(partial_ref, rest_ref, other_ref, codes_ref, cells_ref, wait_ref, out_ref, cells_out):
    cells_out[...] = cells_ref[...]
    flat = (partial_ref[2] + dot(rest_ref[2], other_ref[...], NT)).astype(BF16)
    for head in range(4):
        for b in range(BLK_DEV):
            part = flat[head * 32 : head * 32 + 32, b * BLOCK : (b + 1) * BLOCK]
            out_ref[head, b * 32 : b * 32 + 32, :] = part
        out_ref[head, BLOCK : BLOCK + 16, :] = codes_ref[...]


def spread_kernel(query_ref, *refs):
    out_ref = refs[-1]
    for y in range(4):
        out_ref[y * 4 : y * 4 + 4] = query_ref[...]


def gather_kernel(place_ref, own_ref, *refs):
    *got, out_ref = refs
    for d, ref in enumerate((own_ref, *got)):
        out_ref[(place_ref[3] - d) & 3] = ref[...]


def relay_kernel(left_ref, right_ref, after_ref, low_ref, high_ref, both_ref):
    low_ref[...] = left_ref[:2]
    high_ref[...] = right_ref[2:]
    both_ref[:4] = left_ref[...]
    both_ref[4:] = right_ref[...]


def pass_kernel(low_ref, high_ref, after_ref, out_ref):
    out_ref[:2] = low_ref[...]
    out_ref[2:] = high_ref[...]


def ends_kernel(place_ref, cells_ref, up_ref, down_ref, wait_ref, before_ref, after_ref):
    spot = place_ref[4] * 8 + place_ref[3] * 2 + place_ref[2]
    cells = cells_ref[...]
    before_ref[...] = jnp.where(spot == 31, up_ref[...], cells)
    after_ref[...] = jnp.where(spot == 0, down_ref[...], cells)


def pair_kernel(before_ref, after_ref, out_ref):
    rows = before_ref.shape[0]
    out_ref[:rows, :] = before_ref[...]
    out_ref[rows:, :] = after_ref[...]


def edge_kernel(
    wb_ref, place_ref, own_ref, other_ref, near_ref, near_other_ref, ws_ref, wt_ref, bias_ref, edge_ref, out_ref, win, tgt
):
    side = place_ref[0]
    rows = own_ref.shape[0]
    whole = whole_rows(side, own_ref[...], other_ref[...])
    for g in range(2):
        tgt[:, g * BLOCK : (g + 1) * BLOCK] = dot(whole, wt_ref[g], NN) + bias_ref[g : g + 1, :]
    for spot, cells in enumerate(
        (
            whole_rows(side, near_ref[:rows, :], near_other_ref[:rows, :]),
            whole,
            whole_rows(side, near_ref[rows:, :], near_other_ref[rows:, :]),
        )
    ):
        for g in range(2):
            source = dot(cells, ws_ref[g], NN).astype(BF16)
            for block in range(BLK_DEV):
                win[spot * BLK_DEV + block, :, g * BLOCK : (g + 1) * BLOCK] = source[block * BLOCK : (block + 1) * BLOCK, :]
    lane = lax.broadcasted_iota(jnp.int32, (BLOCK, 4 * BLOCK), 1)

    def one(block, unused):
        rows = pl.ds(pl.multiple_of(block * BLOCK, BLOCK), BLOCK)
        table = jnp.concatenate([win[wb_ref[block, k]] for k in range(4)], axis=0)
        target = tgt[rows, :]
        picks = edge_ref[rows, :]
        total = jnp.zeros((BLOCK, BLOCK), F32)
        for e in range(8):
            hot = (picks[:, e : e + 1] == lane).astype(F32).astype(BF16)
            pre = dot(hot, table, NN) + target
            gate = 0.5 + 0.5 * jnp.tanh(0.5 * pre[:, :BLOCK])
            value = pre[:, BLOCK:]
            total = total + gate * (value * (0.5 + 0.5 * jnp.tanh(0.5 * value)))
        out_ref[rows, :] = own_ref[rows, :].astype(F32) + total * 0.125
        return unused

    lax.fori_loop(0, BLK_DEV, one, 0)


def load_blocks(pieces, keys, values):
    first = 0
    for ref in pieces:
        for x in range(ref.shape[0]):
            for b in range(BLK_DEV):
                part = ref[x, b * 32 : (b + 1) * 32, :].astype(F32)
                keys[first] = jnp.transpose(part).astype(BF16)
                values[first, 0:32, :] = ref[x, BLOCK + b * 32 : BLOCK + (b + 1) * 32, :]
                values[first, 32:48, :] = jnp.ones((16, BLOCK), BF16)
                first += 1
    keys[first] = jnp.zeros((BLOCK, 32), BF16)
    values[first] = jnp.zeros((48, BLOCK), BF16)


def accumulate(stage, unroll, list_ref, start, end, queries, keys, values, acc, scored):
    base = STAGES[stage][0]
    spare = keys.shape[0] - 1

    def length(i):
        return list_ref[(i >> 2) * 2 + 1, ((i & 3) << 2) + stage]

    def following(i, j):
        over = j + 1 >= length(i)
        return jnp.where(over, jnp.minimum(i + 1, end), i), jnp.where(over, 0, j + 1)

    def batch(i, j):
        units = [(i, j)]
        for _ in range(unroll - 1):
            units.append(following(*units[-1]))
        return units

    def picked(table, axis, i, j):
        row, column = (i >> 2) * 2, ((i & 3) << 5) + base + j * GROUP
        blocks = [jnp.where(i < end, jnp.minimum(list_ref[row, column + g], spare), spare) for g in range(GROUP)]
        return jnp.concatenate([table[block] for block in blocks], axis=axis)

    def scores(units):
        for w, (i, j) in enumerate(units):
            scored[w] = dot(picked(keys, 0, i, j), queries[i - start], NN)

    def step(u, state):
        now = [(state[2 * w], state[2 * w + 1]) for w in range(unroll)]
        later = batch(*following(*now[-1]))
        weights = [jnp.exp2(scored[w] * EXP2_SCALE).astype(BF16) for w in range(unroll)]
        scores(later)
        for w, (i, j) in enumerate(now):
            acc[i - start] = acc[i - start] + dot(picked(values, 1, i, j), weights[w], NN)[0:40, :]
        return tuple(v for pair in later for v in pair)

    count = lax.fori_loop(start, end, lambda i, s: s + length(i), jnp.int32(0))
    begin = batch(jnp.int32(0) + start, jnp.int32(0))
    scores(begin)
    lax.fori_loop(0, (count + unroll - 1) // unroll, step, tuple(v for pair in begin for v in pair))


def attend_kernel(stage, npieces, resume, list_ref, q_ref, *refs):
    last = stage == len(STAGES) - 1
    pieces, refs = refs[:npieces], refs[npieces:]
    out_ref, queries, keys, values, scored, *rest = refs[1:] if resume else refs
    acc = rest[0] if last else out_ref
    for m in range(64):
        top = (m % 4) * 32
        queries[m] = q_ref[m // 16, m // 4 % 4, top : top + 32, :]
    queries[64] = jnp.zeros((32, BLOCK), BF16)
    load_blocks(pieces, keys, values)
    acc[...] = refs[0][...] if resume else jnp.zeros(acc.shape, F32)
    accumulate(stage, UNROLL, list_ref, 0, 64, queries, keys, values, acc, scored)
    if last:
        for y in range(4):
            for m in range(16):
                a = acc[y * 16 + m]
                out_ref[y, m * 32 : (m + 1) * 32, :] = a[0:32, :]
                out_ref[y, 512 + m : 513 + m, :] = a[32:33, :]


def attend(stage, lists, q_all, pieces, carry, flops):
    last = stage == len(STAGES) - 1
    blocks = STAGES[stage][1] * BLK_DEV + 1
    scratch = [
        pltpu.VMEM((65, 32, BLOCK), BF16),
        pltpu.VMEM((blocks, BLOCK, 32), BF16),
        pltpu.VMEM((blocks, 48, BLOCK), BF16),
        pltpu.VMEM((UNROLL, BLOCK * GROUP, BLOCK), F32),
    ]
    if last:
        scratch.append(pltpu.VMEM((65, 40, BLOCK), F32))
    (out,) = call(
        functools.partial(attend_kernel, stage, len(pieces), carry is not None),
        [shaped((4, 528, BLOCK) if last else (65, 40, BLOCK), F32)],
        [q_all, *pieces] + ([] if carry is None else [carry]),
        "attend" + str(stage),
        scalars=(lists,),
        scratch=scratch,
        flops=flops,
    )
    return out


def mix_kernel(part_ref, weight_ref, out_ref):
    total = part_ref[0] + part_ref[1] + part_ref[2] + part_ref[3]
    for m in range(16):
        mixed = (total[m * 32 : (m + 1) * 32, :] / total[512 + m : 513 + m, :]).astype(BF16)
        for peer in range(2):
            out_ref[(m // 4) * 2 + peer, (m % 4) * 32 : (m % 4) * 32 + 32, :] = mixed


def weight_kernel(place_ref, w_mine_ref, w_other_ref, out_ref):
    side = place_ref[0]
    columns = pl.ds(pl.multiple_of(side * BLOCK, BLOCK), BLOCK)
    mine, other = w_mine_ref[:, columns], w_other_ref[:, columns]
    halves = (jnp.where(side == 0, mine, other), jnp.where(side == 0, other, mine))
    out_ref[...] = jnp.concatenate([h[x * 32 : x * 32 + 32, :] for x in range(4) for h in halves], axis=0)


def final_kernel(mixed_ref, weight_ref, base_ref, out_ref):
    for block in range(BLK_DEV):
        rows = slice(block * BLOCK, (block + 1) * BLOCK)
        mixed = jnp.concatenate([mixed_ref[k, block * 32 : block * 32 + 32, :] for k in range(8)], axis=0)
        out_ref[rows, :] = (base_ref[rows, :] + dot(mixed, weight_ref[...], TN)).astype(BF16)


def shaped(shape, dtype):
    return jax.ShapeDtypeStruct(shape, dtype)


def body(cells, w_query, w_key, w_value, w_source, w_target, msg_bias, w_out, nbr_block, edge_src, key_blocks):
    rows = cells.shape[0]
    everyone = ("zh", "y", "x", "c")
    nparts = 128
    mine = lax.axis_index(everyone)
    side = lax.axis_index("h")
    swap = [(0, 1), (1, 0)]
    ring = [[(i, (i + d) % 4) for i in range(4)] for d in range(4)]
    other = lax.ppermute(cells, "h", swap)
    w_got = lax.ppermute(w_out, "h", swap)
    tops = [(z * 32 + 31, (z + 1) % 4 * 32 + 31) for z in range(4)]
    bottoms = [((z + 1) % 4 * 32, z * 32) for z in range(4)]
    places = jnp.stack([side, lax.axis_index("zh"), lax.axis_index("c"), lax.axis_index("x"), lax.axis_index("y")])
    partial, rest, codes = call(
        prepare_kernel,
        [shaped((3, BLOCK, rows), F32), shaped((3, BLOCK, BLOCK), BF16), shaped((16, BLOCK), BF16)],
        [cells, jnp.stack([w_key, w_value, w_query]), key_blocks],
        "prepare",
        scalars=(places,),
    )
    own, *sends = call(
        keyval_kernel,
        [shaped((256, BLOCK), BF16)] * 4,
        [partial, rest, other],
        "keyval",
        scalars=(places,),
        scratch=[pltpu.VMEM((4, 256, BLOCK), BF16)],
    )
    got = [lax.ppermute(v, "x", ring[d + 1]) for d, v in enumerate(sends)]
    (here,) = call(gather_kernel, [shaped((4, 256, BLOCK), BF16)], [own, *got], "gather", scalars=(places,))
    left = lax.ppermute(here, "zh", ring[1])
    right = lax.ppermute(here, "zh", ring[3])
    mate_here = lax.ppermute(here, "c", swap)
    query, passed = call(
        query_kernel,
        [shaped((4, 144, BLOCK), BF16), shaped(cells.shape, BF16)],
        [partial, rest, other, codes, cells],
        "query",
        after=[got[0]],
    )
    up = lax.ppermute(passed, everyone, tops)
    down = lax.ppermute(passed, everyone, bottoms)
    (query,) = call(spread_kernel, [shaped((16, 144, BLOCK), BF16)], [query], "spread", after=[*got, up, down])
    q_all = lax.all_to_all(query, ("y", "x"), 0, 0).reshape(4, 4, 144, BLOCK)
    lists = lax.dynamic_slice_in_dim(q_all, BLOCK + 2 * lax.axis_index("y"), 2, 2)
    lists = jnp.pad(lists.reshape(32, BLOCK).astype(jnp.int32), ((0, 8), (0, 0)), constant_values=EMPTY)
    partial = attend(0, lists, q_all, [here, mate_here], None, 10**6)
    shapes = [shaped((n, 256, BLOCK), BF16) for n in (2, 2, 8)]
    low, high, both = call(relay_kernel, shapes, [left, right], "relay", after=[partial])
    far_low = lax.ppermute(low, "zh", ring[1])
    far_high = lax.ppermute(high, "zh", ring[3])
    partial = attend(1, lists, q_all, [both, lax.ppermute(both, "c", swap)], partial, 9 * 10**9)
    (across,) = call(pass_kernel, [shaped((4, 256, BLOCK), BF16)], [far_low, far_high], "across", after=[partial])
    partial = attend(2, lists, q_all, [across, lax.ppermute(across, "c", swap)], partial, 5 * 10**9)
    plane = [(i, (i + 1) % 32) for i in range(32)]
    ends = [shaped((rows, BLOCK), BF16)] * 2
    before, after = call(ends_kernel, ends, [cells, up, down], "ends", scalars=(places,), after=[partial])
    before = lax.ppermute(before, ("y", "x", "c"), plane)
    after = lax.ppermute(after, ("y", "x", "c"), [(j, i) for i, j in plane])
    (around,) = call(pair_kernel, [shaped((2 * rows, BLOCK), BF16)], [before, after], "around")
    around_other = lax.ppermute(around, "h", swap)
    window_block = (nbr_block // BLK_DEV - mine + 1) % nparts * BLK_DEV + nbr_block % BLK_DEV
    (base,) = call(
        edge_kernel,
        [shaped((rows, BLOCK), F32)],
        [cells, other, around, around_other, w_source, w_target, msg_bias, edge_src],
        "edge",
        scalars=(window_block, places),
        scratch=[pltpu.VMEM((12, BLOCK, 256), BF16), pltpu.VMEM((rows, 256), F32)],
        flops=4 * 10**9,
        trans=10**6,
    )
    (w_full,) = call(weight_kernel, [shaped((256, BLOCK), BF16)], [w_out, w_got], "weight", scalars=(places,))
    (mixed,) = call(mix_kernel, [shaped((8, BLOCK, BLOCK), BF16)], [lax.all_to_all(partial, "y", 0, 0)], "mix", after=[w_full])
    mixed = lax.all_to_all(mixed, ("x", "h"), 0, 0)
    (out,) = call(
        final_kernel, [shaped((rows, BLOCK), BF16)], [mixed, w_full, base], "final"
    )
    return out


def solution(mesh):
    split = Mesh(mesh.devices.reshape(4, 4, 4, 2, 2), ("zh", "y", "x", "c", "h"))
    blk = ("zh", "y", "x", "c")
    in_specs = (
        P(blk, "h"),
        P(None, "h"),
        P(None, "h"),
        P(None, "h"),
        P(None, None, "h"),
        P(None, None, "h"),
        P(None, "h"),
        P("h", None),
        P(blk, None),
        P(blk, None),
        P(blk, None),
    )
    return jax.shard_map(body, mesh=split, in_specs=in_specs, out_specs=P(blk, "h"), check_vma=False)
```

```python
import functools
import math

import jax
import jax.numpy as jnp
from jax import lax
from jax.experimental import pallas as pl
from jax.experimental.pallas import tpu as pltpu
from jax.sharding import Mesh
from jax.sharding import PartitionSpec as P

HEAD_DIM = 32
BLOCK = 128
BLK_DEV = 4
GROUP = 2
UNROLL = 8
EMPTY = 64
STAGES = ((0, 8), (8, 16), (24, 8))
NN = (((1,), (0,)), ((), ()))
NT = (((1,), (1,)), ((), ()))
TN = (((0,), (0,)), ((), ()))
TT = (((0,), (1,)), ((), ()))
F32 = jnp.float32
BF16 = jnp.bfloat16
EXP2_SCALE = math.log2(math.e) / math.sqrt(HEAD_DIM)


def dot(a, b, dims):
    return lax.dot_general(a, b, dims, preferred_element_type=F32)


def full(shape):
    return pl.BlockSpec(shape, lambda *_: (0,) * len(shape))


def call(kernel, outs, args, name, scalars=(), scratch=(), flops=10**6, trans=0, after=()):
    moved = sum(a.size * a.dtype.itemsize for a in args)
    return pl.pallas_call(
        kernel,
        grid_spec=pltpu.PrefetchScalarGridSpec(
            num_scalar_prefetch=len(scalars),
            grid=(1,),
            in_specs=[full(a.shape) for a in args] + [pl.BlockSpec(memory_space=pl.ANY)] * len(after),
            out_specs=[full(o.shape) for o in outs],
            scratch_shapes=list(scratch),
        ),
        out_shape=outs,
        compiler_params=pltpu.CompilerParams(vmem_limit_bytes=48 << 20),
        cost_estimate=pl.CostEstimate(flops=flops, bytes_accessed=moved, transcendentals=trans),
        name=name,
    )(*scalars, *args, *after)


def whole_rows(side, own, other):
    first = side == 0
    return jnp.concatenate([jnp.where(first, own, other), jnp.where(first, other, own)], axis=1)


def prepare_kernel(place_ref, cells_ref, weights_ref, blocks_ref, partial_ref, rest_ref, codes_ref):
    side, zh, core = place_ref[0], place_ref[1], place_ref[2]

    def facts(ids):
        owner = ids // BLK_DEV
        far = (owner // 32 - zh) & 3
        stage = jnp.where(far == 0, 0, jnp.where(far == 2, 2, 1))
        mate = jnp.where(stage == 1, 8, 4)
        slot = jnp.where(owner % 2 != core, mate, 0) + owner // 2 % 4 + jnp.where(far == 1, 4, 0)
        return owner // 8 % 4, stage, slot * BLK_DEV + ids % BLK_DEV

    lane = lax.broadcasted_iota(jnp.int32, (32, 32), 1)
    below = lane < lax.broadcasted_iota(jnp.int32, (32, 32), 0)
    found = [[] for _ in range(4)]
    tally = [jnp.zeros((1, 32), F32) for _ in range(4)]
    for block in range(BLK_DEV):
        across = jnp.broadcast_to(blocks_ref[block : block + 1, :], (32, 32))
        down = jnp.transpose(across.astype(F32)).astype(jnp.int32)
        y_across, stage_across, _ = facts(across)
        y_down, stage_down, code = facts(down)
        same = (y_across == y_down) & (stage_across == stage_down) & below
        rank = jnp.sum(same.astype(F32), axis=1, keepdims=True).astype(jnp.int32)
        start = jnp.where(stage_down == 0, 0, jnp.where(stage_down == 1, 8, 24))
        at = rank + start == lane
        for y in range(4):
            row = jnp.sum(jnp.where(at & (y_down == y), code - EMPTY, 0).astype(F32), axis=0, keepdims=True)
            found[y].append(row + EMPTY)
            listed = (y_down == y) & (stage_down + 4 * block == lane)
            tally[y] = tally[y] + jnp.sum(listed.astype(F32), axis=0, keepdims=True)
    rows = []
    for y in range(4):
        units = jnp.maximum((tally[y].astype(jnp.int32) + GROUP - 1) // GROUP, 1).astype(F32)
        rows += [jnp.concatenate(found[y], axis=1), jnp.concatenate([units, jnp.zeros((1, 96), F32)], axis=1)]
    codes_ref[...] = jnp.concatenate(rows + [jnp.zeros((8, BLOCK), F32)], axis=0).astype(BF16)
    mine = pl.ds(pl.multiple_of(side * BLOCK, BLOCK), BLOCK)
    theirs = pl.ds(pl.multiple_of((1 - side) * BLOCK, BLOCK), BLOCK)
    for n in range(3):
        partial_ref[n] = dot(weights_ref[n, mine, :], cells_ref[...], TT)
        rest_ref[n] = jnp.transpose(weights_ref[n, theirs, :].astype(F32)).astype(BF16)


def keyval_kernel(place_ref, partial_ref, rest_ref, other_ref, own_ref, *outs):
    *sends, keyval = outs
    other = other_ref[...]
    for n in range(2):
        flat = (partial_ref[n] + dot(rest_ref[n], other, NT)).astype(BF16)
        for head in range(4):
            ahead = (head - place_ref[3]) & 3
            for b in range(BLK_DEV):
                part = flat[head * 32 : head * 32 + 32, b * BLOCK : (b + 1) * BLOCK]
                keyval[ahead, n * BLOCK + b * 32 : n * BLOCK + b * 32 + 32, :] = part
    own_ref[...] = keyval[0]
    for d, ref in enumerate(sends):
        ref[...] = keyval[d + 1]


def query_kernel(partial_ref, rest_ref, other_ref, codes_ref, out_ref):
    flat = (partial_ref[2] + dot(rest_ref[2], other_ref[...], NT)).astype(BF16)
    for head in range(4):
        for b in range(BLK_DEV):
            part = flat[head * 32 : head * 32 + 32, b * BLOCK : (b + 1) * BLOCK]
            out_ref[head, b * 32 : b * 32 + 32, :] = part
        out_ref[head, BLOCK : BLOCK + 16, :] = codes_ref[...]


def spread_kernel(query_ref, *refs):
    out_ref = refs[-1]
    for y in range(4):
        out_ref[y * 4 : y * 4 + 4] = query_ref[...]


def gather_kernel(place_ref, own_ref, *refs):
    *got, out_ref = refs
    for d, ref in enumerate((own_ref, *got)):
        out_ref[(place_ref[3] - d) & 3] = ref[...]


def relay_kernel(left_ref, right_ref, after_ref, low_ref, high_ref, both_ref):
    low_ref[...] = left_ref[:2]
    high_ref[...] = right_ref[2:]
    both_ref[:4] = left_ref[...]
    both_ref[4:] = right_ref[...]


def pass_kernel(low_ref, high_ref, after_ref, out_ref):
    out_ref[:2] = low_ref[...]
    out_ref[2:] = high_ref[...]


def ends_kernel(place_ref, cells_ref, up_ref, down_ref, wait_ref, before_ref, after_ref):
    spot = place_ref[4] * 8 + place_ref[3] * 2 + place_ref[2]
    cells = cells_ref[...]
    before_ref[...] = jnp.where(spot == 31, up_ref[...], cells)
    after_ref[...] = jnp.where(spot == 0, down_ref[...], cells)


def pair_kernel(before_ref, after_ref, out_ref):
    rows = before_ref.shape[0]
    out_ref[:rows, :] = before_ref[...]
    out_ref[rows:, :] = after_ref[...]


def edge_kernel(
    wb_ref, place_ref, own_ref, other_ref, near_ref, near_other_ref, ws_ref, wt_ref, bias_ref, edge_ref, out_ref, win, tgt
):
    side = place_ref[0]
    rows = own_ref.shape[0]
    whole = whole_rows(side, own_ref[...], other_ref[...])
    for g in range(2):
        tgt[:, g * BLOCK : (g + 1) * BLOCK] = dot(whole, wt_ref[g], NN) + bias_ref[g : g + 1, :]
    for spot, cells in enumerate(
        (
            whole_rows(side, near_ref[:rows, :], near_other_ref[:rows, :]),
            whole,
            whole_rows(side, near_ref[rows:, :], near_other_ref[rows:, :]),
        )
    ):
        for g in range(2):
            source = dot(cells, ws_ref[g], NN).astype(BF16)
            for block in range(BLK_DEV):
                win[spot * BLK_DEV + block, :, g * BLOCK : (g + 1) * BLOCK] = source[block * BLOCK : (block + 1) * BLOCK, :]
    lane = lax.broadcasted_iota(jnp.int32, (BLOCK, 4 * BLOCK), 1)

    def one(block, unused):
        rows = pl.ds(pl.multiple_of(block * BLOCK, BLOCK), BLOCK)
        table = jnp.concatenate([win[wb_ref[block, k]] for k in range(4)], axis=0)
        target = tgt[rows, :]
        picks = edge_ref[rows, :]
        total = jnp.zeros((BLOCK, BLOCK), F32)
        for e in range(8):
            hot = (picks[:, e : e + 1] == lane).astype(F32).astype(BF16)
            pre = dot(hot, table, NN) + target
            gate = 0.5 + 0.5 * jnp.tanh(0.5 * pre[:, :BLOCK])
            value = pre[:, BLOCK:]
            total = total + gate * (value * (0.5 + 0.5 * jnp.tanh(0.5 * value)))
        out_ref[rows, :] = own_ref[rows, :].astype(F32) + total * 0.125
        return unused

    lax.fori_loop(0, BLK_DEV, one, 0)


def load_blocks(pieces, keys, values):
    first = 0
    for ref in pieces:
        for x in range(ref.shape[0]):
            for b in range(BLK_DEV):
                part = ref[x, b * 32 : (b + 1) * 32, :].astype(F32)
                keys[first] = jnp.transpose(part).astype(BF16)
                values[first, 0:32, :] = ref[x, BLOCK + b * 32 : BLOCK + (b + 1) * 32, :]
                values[first, 32:48, :] = jnp.ones((16, BLOCK), BF16)
                first += 1
    keys[first] = jnp.zeros((BLOCK, 32), BF16)
    values[first] = jnp.zeros((48, BLOCK), BF16)


def accumulate(stage, unroll, list_ref, start, end, queries, keys, values, acc, scored):
    base = STAGES[stage][0]
    spare = keys.shape[0] - 1

    def length(i):
        return list_ref[(i >> 2) * 2 + 1, ((i & 3) << 2) + stage]

    def following(i, j):
        over = j + 1 >= length(i)
        return jnp.where(over, jnp.minimum(i + 1, end), i), jnp.where(over, 0, j + 1)

    def batch(i, j):
        units = [(i, j)]
        for _ in range(unroll - 1):
            units.append(following(*units[-1]))
        return units

    def picked(table, axis, i, j):
        row, column = (i >> 2) * 2, ((i & 3) << 5) + base + j * GROUP
        blocks = [jnp.where(i < end, jnp.minimum(list_ref[row, column + g], spare), spare) for g in range(GROUP)]
        return jnp.concatenate([table[block] for block in blocks], axis=axis)

    def scores(units):
        for w, (i, j) in enumerate(units):
            scored[w] = dot(picked(keys, 0, i, j), queries[i - start], NN)

    def step(u, state):
        now = [(state[2 * w], state[2 * w + 1]) for w in range(unroll)]
        later = batch(*following(*now[-1]))
        weights = [jnp.exp2(scored[w] * EXP2_SCALE).astype(BF16) for w in range(unroll)]
        scores(later)
        for w, (i, j) in enumerate(now):
            acc[i - start] = acc[i - start] + dot(picked(values, 1, i, j), weights[w], NN)[0:40, :]
        return tuple(v for pair in later for v in pair)

    count = lax.fori_loop(start, end, lambda i, s: s + length(i), jnp.int32(0))
    begin = batch(jnp.int32(0) + start, jnp.int32(0))
    scores(begin)
    lax.fori_loop(0, (count + unroll - 1) // unroll, step, tuple(v for pair in begin for v in pair))


def attend_kernel(stage, npieces, resume, list_ref, q_ref, *refs):
    last = stage == len(STAGES) - 1
    pieces, refs = refs[:npieces], refs[npieces:]
    out_ref, queries, keys, values, scored, *rest = refs[1:] if resume else refs
    acc = rest[0] if last else out_ref
    for m in range(64):
        top = (m % 4) * 32
        queries[m] = q_ref[m // 16, m // 4 % 4, top : top + 32, :]
    queries[64] = jnp.zeros((32, BLOCK), BF16)
    load_blocks(pieces, keys, values)
    acc[...] = refs[0][...] if resume else jnp.zeros(acc.shape, F32)
    accumulate(stage, UNROLL, list_ref, 0, 64, queries, keys, values, acc, scored)
    if last:
        for y in range(4):
            for m in range(16):
                a = acc[y * 16 + m]
                out_ref[y, m * 32 : (m + 1) * 32, :] = a[0:32, :]
                out_ref[y, 512 + m : 513 + m, :] = a[32:33, :]


def attend(stage, lists, q_all, pieces, carry, flops):
    last = stage == len(STAGES) - 1
    blocks = STAGES[stage][1] * BLK_DEV + 1
    scratch = [
        pltpu.VMEM((65, 32, BLOCK), BF16),
        pltpu.VMEM((blocks, BLOCK, 32), BF16),
        pltpu.VMEM((blocks, 48, BLOCK), BF16),
        pltpu.VMEM((UNROLL, BLOCK * GROUP, BLOCK), F32),
    ]
    if last:
        scratch.append(pltpu.VMEM((65, 40, BLOCK), F32))
    (out,) = call(
        functools.partial(attend_kernel, stage, len(pieces), carry is not None),
        [shaped((4, 528, BLOCK) if last else (65, 40, BLOCK), F32)],
        [q_all, *pieces] + ([] if carry is None else [carry]),
        "attend" + str(stage),
        scalars=(lists,),
        scratch=scratch,
        flops=flops,
    )
    return out


def mix_kernel(part_ref, weight_ref, out_ref):
    total = part_ref[0] + part_ref[1] + part_ref[2] + part_ref[3]
    for m in range(16):
        mixed = (total[m * 32 : (m + 1) * 32, :] / total[512 + m : 513 + m, :]).astype(BF16)
        for peer in range(2):
            out_ref[(m // 4) * 2 + peer, (m % 4) * 32 : (m % 4) * 32 + 32, :] = mixed


def weight_kernel(place_ref, w_mine_ref, w_other_ref, out_ref):
    side = place_ref[0]
    columns = pl.ds(pl.multiple_of(side * BLOCK, BLOCK), BLOCK)
    mine, other = w_mine_ref[:, columns], w_other_ref[:, columns]
    halves = (jnp.where(side == 0, mine, other), jnp.where(side == 0, other, mine))
    out_ref[...] = jnp.concatenate([h[x * 32 : x * 32 + 32, :] for x in range(4) for h in halves], axis=0)


def final_kernel(mixed_ref, weight_ref, base_ref, out_ref):
    for block in range(BLK_DEV):
        rows = slice(block * BLOCK, (block + 1) * BLOCK)
        mixed = jnp.concatenate([mixed_ref[k, block * 32 : block * 32 + 32, :] for k in range(8)], axis=0)
        out_ref[rows, :] = (base_ref[rows, :] + dot(mixed, weight_ref[...], TN)).astype(BF16)


def shaped(shape, dtype):
    return jax.ShapeDtypeStruct(shape, dtype)


def body(cells, w_query, w_key, w_value, w_source, w_target, msg_bias, w_out, nbr_block, edge_src, key_blocks):
    rows = cells.shape[0]
    everyone = ("zh", "y", "x", "c")
    nparts = 128
    mine = lax.axis_index(everyone)
    side = lax.axis_index("h")
    swap = [(0, 1), (1, 0)]
    ring = [[(i, (i + d) % 4) for i in range(4)] for d in range(4)]
    other = lax.ppermute(cells, "h", swap)
    w_got = lax.ppermute(w_out, "h", swap)
    tops = [(z * 32 + 31, (z + 1) % 4 * 32 + 31) for z in range(4)]
    bottoms = [((z + 1) % 4 * 32, z * 32) for z in range(4)]
    up = lax.ppermute(cells, everyone, tops)
    down = lax.ppermute(cells, everyone, bottoms)
    places = jnp.stack([side, lax.axis_index("zh"), lax.axis_index("c"), lax.axis_index("x"), lax.axis_index("y")])
    partial, rest, codes = call(
        prepare_kernel,
        [shaped((3, BLOCK, rows), F32), shaped((3, BLOCK, BLOCK), BF16), shaped((16, BLOCK), BF16)],
        [cells, jnp.stack([w_key, w_value, w_query]), key_blocks],
        "prepare",
        scalars=(places,),
    )
    own, *sends = call(
        keyval_kernel,
        [shaped((256, BLOCK), BF16)] * 4,
        [partial, rest, other],
        "keyval",
        scalars=(places,),
        scratch=[pltpu.VMEM((4, 256, BLOCK), BF16)],
    )
    got = [lax.ppermute(v, "x", ring[d + 1]) for d, v in enumerate(sends)]
    (here,) = call(gather_kernel, [shaped((4, 256, BLOCK), BF16)], [own, *got], "gather", scalars=(places,))
    left = lax.ppermute(here, "zh", ring[1])
    right = lax.ppermute(here, "zh", ring[3])
    mate_here = lax.ppermute(here, "c", swap)
    (query,) = call(query_kernel, [shaped((4, 144, BLOCK), BF16)], [partial, rest, other, codes], "query")
    (query,) = call(spread_kernel, [shaped((16, 144, BLOCK), BF16)], [query], "spread", after=[*got, up, down])
    q_all = lax.all_to_all(query, ("y", "x"), 0, 0).reshape(4, 4, 144, BLOCK)
    lists = lax.dynamic_slice_in_dim(q_all, BLOCK + 2 * lax.axis_index("y"), 2, 2)
    lists = jnp.pad(lists.reshape(32, BLOCK).astype(jnp.int32), ((0, 8), (0, 0)), constant_values=EMPTY)
    partial = attend(0, lists, q_all, [here, mate_here], None, 10**6)
    shapes = [shaped((n, 256, BLOCK), BF16) for n in (2, 2, 8)]
    low, high, both = call(relay_kernel, shapes, [left, right], "relay", after=[partial])
    far_low = lax.ppermute(low, "zh", ring[1])
    far_high = lax.ppermute(high, "zh", ring[3])
    partial = attend(1, lists, q_all, [both, lax.ppermute(both, "c", swap)], partial, 9 * 10**9)
    (across,) = call(pass_kernel, [shaped((4, 256, BLOCK), BF16)], [far_low, far_high], "across", after=[partial])
    partial = attend(2, lists, q_all, [across, lax.ppermute(across, "c", swap)], partial, 5 * 10**9)
    plane = [(i, (i + 1) % 32) for i in range(32)]
    ends = [shaped((rows, BLOCK), BF16)] * 2
    before, after = call(ends_kernel, ends, [cells, up, down], "ends", scalars=(places,), after=[partial])
    before = lax.ppermute(before, ("y", "x", "c"), plane)
    after = lax.ppermute(after, ("y", "x", "c"), [(j, i) for i, j in plane])
    (around,) = call(pair_kernel, [shaped((2 * rows, BLOCK), BF16)], [before, after], "around")
    around_other = lax.ppermute(around, "h", swap)
    window_block = (nbr_block // BLK_DEV - mine + 1) % nparts * BLK_DEV + nbr_block % BLK_DEV
    (base,) = call(
        edge_kernel,
        [shaped((rows, BLOCK), F32)],
        [cells, other, around, around_other, w_source, w_target, msg_bias, edge_src],
        "edge",
        scalars=(window_block, places),
        scratch=[pltpu.VMEM((12, BLOCK, 256), BF16), pltpu.VMEM((rows, 256), F32)],
        flops=4 * 10**9,
        trans=10**6,
    )
    (w_full,) = call(weight_kernel, [shaped((256, BLOCK), BF16)], [w_out, w_got], "weight", scalars=(places,))
    (mixed,) = call(mix_kernel, [shaped((8, BLOCK, BLOCK), BF16)], [lax.all_to_all(partial, "y", 0, 0)], "mix", after=[w_full])
    mixed = lax.all_to_all(mixed, ("x", "h"), 0, 0)
    (out,) = call(
        final_kernel, [shaped((rows, BLOCK), BF16)], [mixed, w_full, base], "final"
    )
    return out


def solution(mesh):
    split = Mesh(mesh.devices.reshape(4, 4, 4, 2, 2), ("zh", "y", "x", "c", "h"))
    blk = ("zh", "y", "x", "c")
    in_specs = (
        P(blk, "h"),
        P(None, "h"),
        P(None, "h"),
        P(None, "h"),
        P(None, None, "h"),
        P(None, None, "h"),
        P(None, "h"),
        P("h", None),
        P(blk, None),
        P(blk, None),
        P(blk, None),
    )
    return jax.shard_map(body, mesh=split, in_specs=in_specs, out_specs=P(blk, "h"), check_vma=False)
```

```python
import functools
import math

import jax
import jax.numpy as jnp
from jax import lax
from jax.experimental import pallas as pl
from jax.experimental.pallas import tpu as pltpu
from jax.sharding import Mesh
from jax.sharding import PartitionSpec as P

HEAD_DIM = 32
BLOCK = 128
BLK_DEV = 4
GROUP = 2
UNROLL = 8
EMPTY = 64
STAGES = ((0, 8), (8, 16), (24, 8))
NN = (((1,), (0,)), ((), ()))
NT = (((1,), (1,)), ((), ()))
TN = (((0,), (0,)), ((), ()))
TT = (((0,), (1,)), ((), ()))
F32 = jnp.float32
BF16 = jnp.bfloat16
EXP2_SCALE = math.log2(math.e) / math.sqrt(HEAD_DIM)


def dot(a, b, dims):
    return lax.dot_general(a, b, dims, preferred_element_type=F32)


def full(shape):
    return pl.BlockSpec(shape, lambda *_: (0,) * len(shape))


def call(kernel, outs, args, name, scalars=(), scratch=(), flops=10**6, trans=0, after=()):
    moved = sum(a.size * a.dtype.itemsize for a in args)
    return pl.pallas_call(
        kernel,
        grid_spec=pltpu.PrefetchScalarGridSpec(
            num_scalar_prefetch=len(scalars),
            grid=(1,),
            in_specs=[full(a.shape) for a in args] + [pl.BlockSpec(memory_space=pl.ANY)] * len(after),
            out_specs=[full(o.shape) for o in outs],
            scratch_shapes=list(scratch),
        ),
        out_shape=outs,
        compiler_params=pltpu.CompilerParams(vmem_limit_bytes=48 << 20),
        cost_estimate=pl.CostEstimate(flops=flops, bytes_accessed=moved, transcendentals=trans),
        name=name,
    )(*scalars, *args, *after)


def whole_rows(side, own, other):
    first = side == 0
    return jnp.concatenate([jnp.where(first, own, other), jnp.where(first, other, own)], axis=1)


def prepare_kernel(place_ref, cells_ref, weights_ref, blocks_ref, partial_ref, rest_ref, codes_ref):
    side, zh, core = place_ref[0], place_ref[1], place_ref[2]

    def facts(ids):
        owner = ids // BLK_DEV
        far = (owner // 32 - zh) & 3
        stage = jnp.where(far == 0, 0, jnp.where(far == 2, 2, 1))
        mate = jnp.where(stage == 1, 8, 4)
        slot = jnp.where(owner % 2 != core, mate, 0) + owner // 2 % 4 + jnp.where(far == 1, 4, 0)
        return owner // 8 % 4, stage, slot * BLK_DEV + ids % BLK_DEV

    lane = lax.broadcasted_iota(jnp.int32, (32, 32), 1)
    below = lane < lax.broadcasted_iota(jnp.int32, (32, 32), 0)
    found = [[] for _ in range(4)]
    tally = [jnp.zeros((1, 32), F32) for _ in range(4)]
    for block in range(BLK_DEV):
        across = jnp.broadcast_to(blocks_ref[block : block + 1, :], (32, 32))
        down = jnp.transpose(across.astype(F32)).astype(jnp.int32)
        y_across, stage_across, _ = facts(across)
        y_down, stage_down, code = facts(down)
        same = (y_across == y_down) & (stage_across == stage_down) & below
        rank = jnp.sum(same.astype(F32), axis=1, keepdims=True).astype(jnp.int32)
        start = jnp.where(stage_down == 0, 0, jnp.where(stage_down == 1, 8, 24))
        at = rank + start == lane
        for y in range(4):
            row = jnp.sum(jnp.where(at & (y_down == y), code - EMPTY, 0).astype(F32), axis=0, keepdims=True)
            found[y].append(row + EMPTY)
            listed = (y_down == y) & (stage_down + 4 * block == lane)
            tally[y] = tally[y] + jnp.sum(listed.astype(F32), axis=0, keepdims=True)
    rows = []
    for y in range(4):
        units = jnp.maximum((tally[y].astype(jnp.int32) + GROUP - 1) // GROUP, 1).astype(F32)
        rows += [jnp.concatenate(found[y], axis=1), jnp.concatenate([units, jnp.zeros((1, 96), F32)], axis=1)]
    codes_ref[...] = jnp.concatenate(rows + [jnp.zeros((8, BLOCK), F32)], axis=0).astype(BF16)
    mine = pl.ds(pl.multiple_of(side * BLOCK, BLOCK), BLOCK)
    theirs = pl.ds(pl.multiple_of((1 - side) * BLOCK, BLOCK), BLOCK)
    for n in range(3):
        partial_ref[n] = dot(weights_ref[n, mine, :], cells_ref[...], TT)
        rest_ref[n] = jnp.transpose(weights_ref[n, theirs, :].astype(F32)).astype(BF16)


def keyval_kernel(place_ref, partial_ref, rest_ref, other_ref, own_ref, *outs):
    *sends, keyval = outs
    other = other_ref[...]
    for n in range(2):
        flat = (partial_ref[n] + dot(rest_ref[n], other, NT)).astype(BF16)
        for head in range(4):
            ahead = (head - place_ref[3]) & 3
            for b in range(BLK_DEV):
                part = flat[head * 32 : head * 32 + 32, b * BLOCK : (b + 1) * BLOCK]
                keyval[ahead, n * BLOCK + b * 32 : n * BLOCK + b * 32 + 32, :] = part
    own_ref[...] = keyval[0]
    for d, ref in enumerate(sends):
        ref[...] = keyval[d + 1]


def query_kernel(partial_ref, rest_ref, other_ref, codes_ref, out_ref):
    flat = (partial_ref[2] + dot(rest_ref[2], other_ref[...], NT)).astype(BF16)
    for head in range(4):
        for b in range(BLK_DEV):
            part = flat[head * 32 : head * 32 + 32, b * BLOCK : (b + 1) * BLOCK]
            out_ref[head, b * 32 : b * 32 + 32, :] = part
        out_ref[head, BLOCK : BLOCK + 16, :] = codes_ref[...]


def spread_kernel(query_ref, *refs):
    out_ref = refs[-1]
    for y in range(4):
        out_ref[y * 4 : y * 4 + 4] = query_ref[...]


def gather_kernel(place_ref, own_ref, *refs):
    *got, out_ref = refs
    for d, ref in enumerate((own_ref, *got)):
        out_ref[(place_ref[3] - d) & 3] = ref[...]


def relay_kernel(left_ref, right_ref, after_ref, up_ref, down_ref, low_ref, high_ref, both_ref):
    low_ref[...] = left_ref[:2]
    high_ref[...] = right_ref[2:]
    both_ref[:4] = left_ref[...]
    both_ref[4:] = right_ref[...]


def across_kernel(low_ref, high_ref, after_ref, out_ref):
    out_ref[:2] = low_ref[...]
    out_ref[2:] = high_ref[...]


def ends_kernel(place_ref, cells_ref, up_ref, down_ref, wait_ref, before_ref, after_ref):
    spot = place_ref[4] * 8 + place_ref[3] * 2 + place_ref[2]
    cells = cells_ref[...]
    before_ref[...] = jnp.where(spot == 31, up_ref[...], cells)
    after_ref[...] = jnp.where(spot == 0, down_ref[...], cells)


def pass_kernel(cells_ref, after_ref, out_ref):
    out_ref[...] = cells_ref[...]


def pair_kernel(before_ref, after_ref, out_ref):
    rows = before_ref.shape[0]
    out_ref[:rows, :] = before_ref[...]
    out_ref[rows:, :] = after_ref[...]


def edge_kernel(
    wb_ref, place_ref, own_ref, other_ref, near_ref, near_other_ref, ws_ref, wt_ref, bias_ref, edge_ref, out_ref, win, tgt
):
    side = place_ref[0]
    rows = own_ref.shape[0]
    whole = whole_rows(side, own_ref[...], other_ref[...])
    for g in range(2):
        tgt[:, g * BLOCK : (g + 1) * BLOCK] = dot(whole, wt_ref[g], NN) + bias_ref[g : g + 1, :]
    for spot, cells in enumerate(
        (
            whole_rows(side, near_ref[:rows, :], near_other_ref[:rows, :]),
            whole,
            whole_rows(side, near_ref[rows:, :], near_other_ref[rows:, :]),
        )
    ):
        for g in range(2):
            source = dot(cells, ws_ref[g], NN).astype(BF16)
            for block in range(BLK_DEV):
                win[spot * BLK_DEV + block, :, g * BLOCK : (g + 1) * BLOCK] = source[block * BLOCK : (block + 1) * BLOCK, :]
    lane = lax.broadcasted_iota(jnp.int32, (BLOCK, 4 * BLOCK), 1)

    def one(block, unused):
        rows = pl.ds(pl.multiple_of(block * BLOCK, BLOCK), BLOCK)
        table = jnp.concatenate([win[wb_ref[block, k]] for k in range(4)], axis=0)
        target = tgt[rows, :]
        picks = edge_ref[rows, :]
        total = jnp.zeros((BLOCK, BLOCK), F32)
        for e in range(8):
            hot = (picks[:, e : e + 1] == lane).astype(F32).astype(BF16)
            pre = dot(hot, table, NN) + target
            gate = 0.5 + 0.5 * jnp.tanh(0.5 * pre[:, :BLOCK])
            value = pre[:, BLOCK:]
            total = total + gate * (value * (0.5 + 0.5 * jnp.tanh(0.5 * value)))
        out_ref[rows, :] = own_ref[rows, :].astype(F32) + total * 0.125
        return unused

    lax.fori_loop(0, BLK_DEV, one, 0)


def load_blocks(pieces, keys, values):
    first = 0
    for ref in pieces:
        for x in range(ref.shape[0]):
            for b in range(BLK_DEV):
                part = ref[x, b * 32 : (b + 1) * 32, :].astype(F32)
                keys[first] = jnp.transpose(part).astype(BF16)
                values[first, 0:32, :] = ref[x, BLOCK + b * 32 : BLOCK + (b + 1) * 32, :]
                values[first, 32:48, :] = jnp.ones((16, BLOCK), BF16)
                first += 1
    keys[first] = jnp.zeros((BLOCK, 32), BF16)
    values[first] = jnp.zeros((48, BLOCK), BF16)


def accumulate(stage, unroll, list_ref, start, end, queries, keys, values, acc, scored):
    base = STAGES[stage][0]
    spare = keys.shape[0] - 1

    def length(i):
        return list_ref[(i >> 2) * 2 + 1, ((i & 3) << 2) + stage]

    def following(i, j):
        over = j + 1 >= length(i)
        return jnp.where(over, jnp.minimum(i + 1, end), i), jnp.where(over, 0, j + 1)

    def batch(i, j):
        units = [(i, j)]
        for _ in range(unroll - 1):
            units.append(following(*units[-1]))
        return units

    def picked(table, axis, i, j):
        row, column = (i >> 2) * 2, ((i & 3) << 5) + base + j * GROUP
        blocks = [jnp.where(i < end, jnp.minimum(list_ref[row, column + g], spare), spare) for g in range(GROUP)]
        return jnp.concatenate([table[block] for block in blocks], axis=axis)

    def scores(units):
        for w, (i, j) in enumerate(units):
            scored[w] = dot(picked(keys, 0, i, j), queries[i - start], NN)

    def step(u, state):
        now = [(state[2 * w], state[2 * w + 1]) for w in range(unroll)]
        later = batch(*following(*now[-1]))
        weights = [jnp.exp2(scored[w] * EXP2_SCALE).astype(BF16) for w in range(unroll)]
        scores(later)
        for w, (i, j) in enumerate(now):
            acc[i - start] = acc[i - start] + dot(picked(values, 1, i, j), weights[w], NN)[0:40, :]
        return tuple(v for pair in later for v in pair)

    count = lax.fori_loop(start, end, lambda i, s: s + length(i), jnp.int32(0))
    begin = batch(jnp.int32(0) + start, jnp.int32(0))
    scores(begin)
    lax.fori_loop(0, (count + unroll - 1) // unroll, step, tuple(v for pair in begin for v in pair))


def attend_kernel(stage, npieces, resume, list_ref, q_ref, *refs):
    last = stage == len(STAGES) - 1
    pieces, refs = refs[:npieces], refs[npieces:]
    out_ref, queries, keys, values, scored, *rest = refs[1:] if resume else refs
    acc = rest[0] if last else out_ref
    for m in range(64):
        top = (m % 4) * 32
        queries[m] = q_ref[m // 16, m // 4 % 4, top : top + 32, :]
    queries[64] = jnp.zeros((32, BLOCK), BF16)
    load_blocks(pieces, keys, values)
    acc[...] = refs[0][...] if resume else jnp.zeros(acc.shape, F32)
    accumulate(stage, UNROLL, list_ref, 0, 64, queries, keys, values, acc, scored)
    if last:
        for y in range(4):
            for m in range(16):
                a = acc[y * 16 + m]
                out_ref[y, m * 32 : (m + 1) * 32, :] = a[0:32, :]
                out_ref[y, 512 + m : 513 + m, :] = a[32:33, :]


def attend(stage, lists, q_all, pieces, carry, flops):
    last = stage == len(STAGES) - 1
    blocks = STAGES[stage][1] * BLK_DEV + 1
    scratch = [
        pltpu.VMEM((65, 32, BLOCK), BF16),
        pltpu.VMEM((blocks, BLOCK, 32), BF16),
        pltpu.VMEM((blocks, 48, BLOCK), BF16),
        pltpu.VMEM((UNROLL, BLOCK * GROUP, BLOCK), F32),
    ]
    if last:
        scratch.append(pltpu.VMEM((65, 40, BLOCK), F32))
    (out,) = call(
        functools.partial(attend_kernel, stage, len(pieces), carry is not None),
        [shaped((4, 528, BLOCK) if last else (65, 40, BLOCK), F32)],
        [q_all, *pieces] + ([] if carry is None else [carry]),
        "attend" + str(stage),
        scalars=(lists,),
        scratch=scratch,
        flops=flops,
    )
    return out


def mix_kernel(part_ref, weight_ref, out_ref):
    total = part_ref[0] + part_ref[1] + part_ref[2] + part_ref[3]
    for m in range(16):
        mixed = (total[m * 32 : (m + 1) * 32, :] / total[512 + m : 513 + m, :]).astype(BF16)
        for peer in range(2):
            out_ref[(m // 4) * 2 + peer, (m % 4) * 32 : (m % 4) * 32 + 32, :] = mixed


def weight_kernel(place_ref, w_mine_ref, w_other_ref, out_ref):
    side = place_ref[0]
    columns = pl.ds(pl.multiple_of(side * BLOCK, BLOCK), BLOCK)
    mine, other = w_mine_ref[:, columns], w_other_ref[:, columns]
    halves = (jnp.where(side == 0, mine, other), jnp.where(side == 0, other, mine))
    out_ref[...] = jnp.concatenate([h[x * 32 : x * 32 + 32, :] for x in range(4) for h in halves], axis=0)


def final_kernel(mixed_ref, weight_ref, base_ref, out_ref):
    for block in range(BLK_DEV):
        rows = slice(block * BLOCK, (block + 1) * BLOCK)
        mixed = jnp.concatenate([mixed_ref[k, block * 32 : block * 32 + 32, :] for k in range(8)], axis=0)
        out_ref[rows, :] = (base_ref[rows, :] + dot(mixed, weight_ref[...], TN)).astype(BF16)


def shaped(shape, dtype):
    return jax.ShapeDtypeStruct(shape, dtype)


def body(cells, w_query, w_key, w_value, w_source, w_target, msg_bias, w_out, nbr_block, edge_src, key_blocks):
    rows = cells.shape[0]
    everyone = ("zh", "y", "x", "c")
    nparts = 128
    mine = lax.axis_index(everyone)
    side = lax.axis_index("h")
    swap = [(0, 1), (1, 0)]
    ring = [[(i, (i + d) % 4) for i in range(4)] for d in range(4)]
    other = lax.ppermute(cells, "h", swap)
    w_got = lax.ppermute(w_out, "h", swap)
    tops = [(z * 32 + 31, (z + 1) % 4 * 32 + 31) for z in range(4)]
    bottoms = [((z + 1) % 4 * 32, z * 32) for z in range(4)]
    places = jnp.stack([side, lax.axis_index("zh"), lax.axis_index("c"), lax.axis_index("x"), lax.axis_index("y")])
    partial, rest, codes = call(
        prepare_kernel,
        [shaped((3, BLOCK, rows), F32), shaped((3, BLOCK, BLOCK), BF16), shaped((16, BLOCK), BF16)],
        [cells, jnp.stack([w_key, w_value, w_query]), key_blocks],
        "prepare",
        scalars=(places,),
    )
    own, *sends = call(
        keyval_kernel,
        [shaped((256, BLOCK), BF16)] * 4,
        [partial, rest, other],
        "keyval",
        scalars=(places,),
        scratch=[pltpu.VMEM((4, 256, BLOCK), BF16)],
    )
    got = [lax.ppermute(v, "x", ring[d + 1]) for d, v in enumerate(sends)]
    (here,) = call(gather_kernel, [shaped((4, 256, BLOCK), BF16)], [own, *got], "gather", scalars=(places,))
    left = lax.ppermute(here, "zh", ring[1])
    right = lax.ppermute(here, "zh", ring[3])
    mate_here = lax.ppermute(here, "c", swap)
    (passed,) = call(pass_kernel, [shaped(cells.shape, BF16)], [cells], "passed", after=[mate_here])
    up = lax.ppermute(passed, everyone, tops)
    down = lax.ppermute(passed, everyone, bottoms)
    (query,) = call(query_kernel, [shaped((4, 144, BLOCK), BF16)], [partial, rest, other, codes], "query")
    (query,) = call(spread_kernel, [shaped((16, 144, BLOCK), BF16)], [query], "spread", after=got)
    q_all = lax.all_to_all(query, ("y", "x"), 0, 0).reshape(4, 4, 144, BLOCK)
    lists = lax.dynamic_slice_in_dim(q_all, BLOCK + 2 * lax.axis_index("y"), 2, 2)
    lists = jnp.pad(lists.reshape(32, BLOCK).astype(jnp.int32), ((0, 8), (0, 0)), constant_values=EMPTY)
    partial = attend(0, lists, q_all, [here, mate_here], None, 10**6)
    shapes = [shaped((n, 256, BLOCK), BF16) for n in (2, 2, 8)]
    low, high, both = call(relay_kernel, shapes, [left, right], "relay", after=[partial, up, down])
    far_low = lax.ppermute(low, "zh", ring[1])
    far_high = lax.ppermute(high, "zh", ring[3])
    partial = attend(1, lists, q_all, [both, lax.ppermute(both, "c", swap)], partial, 9 * 10**9)
    (across,) = call(across_kernel, [shaped((4, 256, BLOCK), BF16)], [far_low, far_high], "across", after=[partial])
    partial = attend(2, lists, q_all, [across, lax.ppermute(across, "c", swap)], partial, 5 * 10**9)
    plane = [(i, (i + 1) % 32) for i in range(32)]
    ends = [shaped((rows, BLOCK), BF16)] * 2
    before, after = call(ends_kernel, ends, [cells, up, down], "ends", scalars=(places,), after=[partial])
    before = lax.ppermute(before, ("y", "x", "c"), plane)
    after = lax.ppermute(after, ("y", "x", "c"), [(j, i) for i, j in plane])
    (around,) = call(pair_kernel, [shaped((2 * rows, BLOCK), BF16)], [before, after], "around")
    around_other = lax.ppermute(around, "h", swap)
    window_block = (nbr_block // BLK_DEV - mine + 1) % nparts * BLK_DEV + nbr_block % BLK_DEV
    (base,) = call(
        edge_kernel,
        [shaped((rows, BLOCK), F32)],
        [cells, other, around, around_other, w_source, w_target, msg_bias, edge_src],
        "edge",
        scalars=(window_block, places),
        scratch=[pltpu.VMEM((12, BLOCK, 256), BF16), pltpu.VMEM((rows, 256), F32)],
        flops=4 * 10**9,
        trans=10**6,
    )
    (w_full,) = call(weight_kernel, [shaped((256, BLOCK), BF16)], [w_out, w_got], "weight", scalars=(places,))
    (mixed,) = call(mix_kernel, [shaped((8, BLOCK, BLOCK), BF16)], [lax.all_to_all(partial, "y", 0, 0)], "mix", after=[w_full])
    mixed = lax.all_to_all(mixed, ("x", "h"), 0, 0)
    (out,) = call(
        final_kernel, [shaped((rows, BLOCK), BF16)], [mixed, w_full, base], "final"
    )
    return out


def solution(mesh):
    split = Mesh(mesh.devices.reshape(4, 4, 4, 2, 2), ("zh", "y", "x", "c", "h"))
    blk = ("zh", "y", "x", "c")
    in_specs = (
        P(blk, "h"),
        P(None, "h"),
        P(None, "h"),
        P(None, "h"),
        P(None, None, "h"),
        P(None, None, "h"),
        P(None, "h"),
        P("h", None),
        P(blk, None),
        P(blk, None),
        P(blk, None),
    )
    return jax.shard_map(body, mesh=split, in_specs=in_specs, out_specs=P(blk, "h"), check_vma=False)
```
